256 devices in a mesh: particle: 8 (over x, z_hi), domain: 32 (over z_lo, y, core).
Axes of the slice: x: 4, y: 4, z: 8 (z_hi: 2, z_lo: 4; z = z_hi * 4 + z_lo), core: 2. Of those that a mesh axis runs over, the one named last changes fastest.
Arguments:
- states: float32 [32, 20, 256, 1024], P('particle', None, 'domain'), may hold values from -6 to 6
- parents: int32 [32], P('particle'), may hold values from 0 to 31
- perturbation: float32 [32, 20, 256, 1024], P('particle', None, 'domain'), may hold values from -4 to 4
- sea_mask: int32 [256, 1024], P('domain'), may hold values 0 or 1
- diffusivity: float32 [20], replicated, may hold values from 0.02 to 0.24
- coupling: float32 [20, 20], replicated, may hold values from -1.25 to 1.25
Outputs:
- forecast: float32 [32, 20, 256, 1024], P('particle', None, 'domain')
The draws below stay inside these ranges and needn't reach their ends.
All inputs are finite; a program needn't handle non-finite values. No bound on the sum of `sea_mask` on one device may be relied on, other than what follows from the above.
Results may differ from the reference program's by a relative error of at most 0.00009.
Values sent between devices are 32-bit elements; how exact they have to be, the bound alone decides.
A program may use at most 128 MiB of HBM per device.

```python
import math
import jax
import jax.numpy as jnp
import numpy as np
from jax import lax

CH = 20
PARTICLES = 32
LON = 1024
NROWS = 256


def touch_ends(result, key, smallest, largest):
    spot = [jax.random.randint(jax.random.fold_in(key, axis), (), 0, length) for axis, length in enumerate(result.shape)]
    main_axis = result.shape.index(max(result.shape))
    neighbour = spot[:main_axis] + [(spot[main_axis] + 1) % result.shape[main_axis]] + spot[main_axis + 1:]
    return result.at[tuple(spot)].set(smallest).at[tuple(neighbour)].set(largest)


def block_scale(stream_key, shape, pieces, least, top_value):
    level, own = 1.0, jax.random.fold_in(stream_key, 6)
    for axis_at, shards_of in pieces:
        draws = jnp.exp(jax.random.uniform(jax.random.fold_in(own, axis_at), (shards_of,), jnp.float32, least / len(pieces), top_value / len(pieces)))
        level = level * jnp.repeat(draws, shape[axis_at] // shards_of).reshape([-1 if axis == axis_at else 1 for axis in range(len(shape))])
    return level


def rank_table(count, lean):
    portions = [(1 << 20) // math.isqrt(rank ** lean) + 1 for rank in range(1, count + 1)]
    deviation = 1 + sum(portions) // (1 << 30)
    return np.cumsum(np.array([max(1, weight // deviation) for weight in portions]))


def skewed_ids(key, dims, number_of, slope):
    listing = rank_table(number_of, slope)
    pick = jax.random.randint(jax.random.fold_in(key, 1), dims, 0, int(listing[number_of - 1]))
    standing = jnp.searchsorted(jnp.asarray(listing, jnp.int32), pick, side="right")
    return jax.random.permutation(jax.random.fold_in(key, 2), number_of)[standing].astype(jnp.int32)


def centred(stream_key, shape, deviation, limit, cuts=(), kind=jnp.bfloat16):
    array = jax.random.normal(stream_key, shape, jnp.float32) * deviation
    if len(cuts) > 0:
        array = block_scale(stream_key, shape, cuts, -0.22, 0.18) * array
    return jnp.clip(array, min=-limit, max=limit).astype(kind)


def setup_inputs(seed: int = 0) -> dict:
    key_list = jax.random.split(jax.random.key(seed), 7)
    return {
        "states": centred(key_list[0], (PARTICLES, CH, NROWS, LON), 1.0, 6.0, ((0, 8), (2, 32)), jnp.float32),
        "parents": touch_ends(skewed_ids(key_list[1], (PARTICLES,), PARTICLES, 2), jax.random.fold_in(key_list[1], 3), 0, PARTICLES - 1).astype(jnp.int32),
        "perturbation": centred(key_list[2], (PARTICLES, CH, NROWS, LON), 0.5, 4.0, ((0, 8), (2, 32)), jnp.float32),
        "sea_mask": touch_ends((jax.random.randint(key_list[3], (NROWS, LON), 0, 10) < 7).astype(jnp.int32), jax.random.fold_in(key_list[3], 1), 0, 1),
        "diffusivity": jnp.clip(jnp.exp(jax.random.uniform(key_list[4], (CH,), jnp.float32, math.log(0.02), math.log(0.24))), 0.02, 0.24),
        "coupling": centred(key_list[5], (CH, CH), CH ** -0.5, 1.25, (), jnp.float32),
    }


def advance(padded, mask_rows, diffusivity, coupling):
    center = padded[:, :, 1:-1]
    laplace = padded[:, :, :-2] + padded[:, :, 2:] + jnp.roll(center, 1, 3) + jnp.roll(center, -1, 3) - 4.0 * center
    coupled = jnp.einsum("cd,pdrl->pcrl", coupling, center, precision=lax.Precision.HIGHEST)
    return center + mask_rows[None, None] * (diffusivity[None, :, None, None] * laplace + coupled)


def with_rims(fields):
    return jnp.pad(fields, ((0, 0), (0, 0), (1, 1), (0, 0)))


def reference(states, parents, perturbation, sea_mask, diffusivity, coupling):
    resampled = jnp.take(states, parents.astype(jnp.int32), axis=0) + perturbation
    mask_rows = sea_mask.astype(jnp.float32)
    first = advance(with_rims(resampled), mask_rows, diffusivity, coupling)
    return advance(with_rims(first), mask_rows, diffusivity, coupling)
```

```python
import functools
import jax
import jax.numpy as jnp
from jax import lax
from jax.experimental import pallas as pl
from jax.experimental.pallas import tpu as pltpu
from jax.sharding import PartitionSpec as P

MESH = pl.DeviceIdType.MESH
CH, LON, ROWS = 20, 1024, 8
GROUP = 5
HALF = 16
CAP = 8
CHUNKS = 8
WIDTH = LON // CHUNKS
AHEAD = 3
WIN = 24


def route(states, pert, parents, mask, res, halo, mask_halo, flag, *scratch):
    it = iter(scratch)
    take = lambda: [next(it) for _ in range(CHUNKS)]
    mine, crossing, crossed, back, got = take(), take(), take(), take(), take()
    edge = take()
    (pert_v, strip, par_send, par_x, par_z, par_xs, par_zs, bits, table, listed) = (next(it) for _ in range(10))
    (s_x1, r_x1, l_x1, s_z, r_z, s_x2, r_x2, s_h, r_h, s_p, r_p, s_q, r_q, s_m, r_m, l_c) = (
        next(it) for _ in range(16)
    )
    p, dom = lax.axis_index("particle"), lax.axis_index("domain")
    x, h = lax.div(p, 2), lax.rem(p, 2)
    peer_x = [lax.rem(x + d, 4) for d in range(4)]
    peers = [(peer_x[d] * 2 + h, dom) for d in range(4)]
    partner = (x * 2 + 1 - h, dom)
    below, above = (p, lax.rem(dom + 31, 32)), (p, lax.rem(dom + 1, 32))

    def remote(src, dst, ss, rs, dev):
        return pltpu.make_async_remote_copy(
            src_ref=src, dst_ref=dst, send_sem=ss, recv_sem=rs, device_id=dev, device_id_type=MESH
        )

    lon = lambda k: pl.ds(k * WIDTH, WIDTH)
    chan = lambda g: pl.ds(g * GROUP, GROUP)

    def x1(k):
        return [
            remote(
                states.at[:, chan(peer_x[d]), :, lon(k)],
                mine[k].at[pl.ds(x * 4, 4)],
                s_x1.at[k, d - 1],
                r_x1.at[k, d - 1],
                peers[d],
            )
            for d in range(1, 4)
        ]

    own = [
        pltpu.make_async_copy(
            states.at[:, chan(x), :, lon(k)], mine[k].at[pl.ds(x * 4, 4)], l_x1.at[k]
        )
        for k in range(CHUNKS)
    ]
    pert_copy = pltpu.make_async_copy(pert, pert_v, l_c.at[0])
    pert_copy.start()
    for k in range(CHUNKS):
        own[k].start()

    lane = lax.broadcasted_iota(jnp.int32, (8, 128), 1)
    row = jnp.zeros((8, 128), jnp.int32)
    for i in range(4):
        row = jnp.where(lane == i, parents[i], row)
    par_send[...] = row
    par_x[pl.ds(x, 1)] = row[None]

    barrier = pltpu.get_barrier_semaphore()
    for dev in peers[1:] + [partner, below, above]:
        pl.semaphore_signal(barrier, inc=1, device_id=dev, device_id_type=MESH)
    pl.semaphore_wait(barrier, 6)

    sent = []

    def go(copies):
        for c in copies:
            c.start()
        sent.extend(copies)
        return copies

    par = go([remote(par_send, par_x.at[x], s_p.at[d - 1], r_p.at[d - 1], peers[d]) for d in range(1, 4)])
    first = {k: go(x1(k)) for k in range(AHEAD)}
    masks = go(
        [
            remote(mask, mask_halo.at[1], s_m.at[0], r_m.at[0], below),
            remote(mask, mask_halo.at[0], s_m.at[1], r_m.at[1], above),
        ]
    )
    for c in par:
        c.wait_recv()
    (par2,) = go([remote(par_x, par_z, s_q.at[0], r_q.at[0], partner)])
    to_smem = pltpu.make_async_copy(par_x, par_xs, l_c.at[1])
    to_smem.start()

    def set_bit(i, b):
        bits[i] = b
        return b + b

    lax.fori_loop(0, 32, set_bit, jnp.int32(1))
    to_smem.wait()
    par2.wait_recv()
    to_smem2 = pltpu.make_async_copy(par_z, par_zs, l_c.at[2])
    to_smem2.start()
    to_smem2.wait()

    def union(ref):
        return lax.fori_loop(
            0, HALF, lambda i, m: m | bits[ref[lax.div(i, 4), 0, lax.rem(i, 4)]], jnp.int32(0)
        )

    wanted_here, wanted_there = union(par_xs), union(par_zs)

    def scan(l, carry):
        n_out, n_in, out = carry
        base = lax.div(l, 4) * 8 + lax.rem(l, 4)
        here, there = base + h * 4, base + (1 - h) * 4
        out_bit = lax.shift_right_logical(wanted_there, here) & 1
        in_bit = lax.shift_right_logical(wanted_here, there) & 1
        table[here] = l
        table[there] = HALF + jnp.minimum(n_in, CAP - 1)
        out = tuple(
            jnp.where((out_bit == 1) & (n_out == c), l, old) for c, old in enumerate(out)
        )
        return n_out + out_bit, n_in + in_bit, out

    zero = jnp.int32(0)
    n_out, n_in, out = lax.fori_loop(0, HALF, scan, (zero, zero, (zero,) * CAP))
    for c in range(CAP):
        listed[c] = out[c]
    flag[0] = jnp.where((n_out > CAP) | (n_in > CAP), 1, 0).astype(jnp.int32)

    res4 = res.reshape(4, CH, ROWS, LON)
    strip4 = strip.reshape(4, CH, ROWS, WIDTH)
    z, second, halos = {}, {}, {}
    for t in range(CHUNKS + 2):
        if t < CHUNKS:
            k = t
            own[k].wait()
            for c in first[k]:
                c.wait_recv()

            def stage_z(c, carry, k=k):
                crossing[k][c] = mine[k][listed[c]]
                return carry

            lax.fori_loop(0, CAP, stage_z, 0)
            z[k] = go([remote(crossing[k], crossed[k], s_z.at[k], r_z.at[k], partner)])
            if k + AHEAD < CHUNKS:
                first[k + AHEAD] = go(x1(k + AHEAD))
        if 1 <= t <= CHUNKS:
            k = t - 1
            z[k][0].wait_recv()
            second[k] = []
            for d in (1, 2, 3, 0):

                def stage_x(j, carry, k=k, d=d):
                    s = table[par_xs[peer_x[d], 0, j]]
                    far = s >= HALF
                    a = mine[k][jnp.where(far, 0, s)]
                    b = crossed[k][jnp.where(far, s - HALF, 0)]
                    v = jnp.where(far, b, a)
                    if d == 0:
                        got[k][x, j] = v
                    else:
                        back[k][d - 1, j] = v
                    return carry

                lax.fori_loop(0, 4, stage_x, 0)
                if d:
                    second[k] += go(
                        [
                            remote(
                                back[k].at[d - 1],
                                got[k].at[x],
                                s_x2.at[k, d - 1],
                                r_x2.at[k, d - 1],
                                peers[d],
                            )
                        ]
                    )
        if t >= 2:
            k = t - 2
            if k == 0:
                pert_copy.wait()
            for c in second[k]:
                c.wait_recv()
            for g in range(4):
                new = got[k][g] + pert_v[:, chan(g), :, lon(k)]
                res4[:, chan(g), :, lon(k)] = new
                strip4[:, chan(g)] = new
            for i, r in enumerate((0, 1, 6, 7)):
                edge[k][i // 2, i % 2] = strip[pl.ds(r, 4 * CH, stride=ROWS)]
            halos[k] = go(
                [
                    remote(edge[k].at[0], halo.at[1, :, :, lon(k)], s_h.at[k, 0], r_h.at[k, 0], below),
                    remote(edge[k].at[1], halo.at[0, :, :, lon(k)], s_h.at[k, 1], r_h.at[k, 1], above),
                ]
            )
    for c in masks:
        c.wait_recv()
    for k in range(CHUNKS):
        for c in halos[k]:
            c.wait_recv()
    for c in sent:
        c.wait_send()


def routed(states, pert, parents, mask):
    dma = pltpu.SemaphoreType.DMA
    vm = lambda *s: pltpu.VMEM(s, jnp.float32)
    scratch = []
    for shape in (
        (HALF, GROUP, ROWS, WIDTH),
        (CAP, GROUP, ROWS, WIDTH),
        (CAP, GROUP, ROWS, WIDTH),
        (3, 4, GROUP, ROWS, WIDTH),
        (4, 4, GROUP, ROWS, WIDTH),
        (2, 2, 4 * CH, WIDTH),
    ):
        scratch += [vm(*shape)] * CHUNKS
    scratch += [
        vm(4, CH, ROWS, LON),
        vm(4 * CH * ROWS, WIDTH),
        pltpu.VMEM((8, 128), jnp.int32),
        pltpu.VMEM((4, 8, 128), jnp.int32),
        pltpu.VMEM((4, 8, 128), jnp.int32),
        pltpu.SMEM((4, 8, 128), jnp.int32),
        pltpu.SMEM((4, 8, 128), jnp.int32),
        pltpu.SMEM((32,), jnp.int32),
        pltpu.SMEM((32,), jnp.int32),
        pltpu.SMEM((CAP,), jnp.int32),
    ]
    three, two, one = dma((CHUNKS, 3)), dma((CHUNKS, 2)), dma((CHUNKS,))
    scratch += [three, three, one, one, one, three, three, two, two, dma((3,)), dma((3,)), dma((1,)), dma((1,)), dma((2,)), dma((2,)), dma((3,))]
    vmem = pl.BlockSpec(memory_space=pltpu.VMEM)
    smem = pl.BlockSpec(memory_space=pltpu.SMEM)
    hbm = pl.BlockSpec(memory_space=pl.ANY)
    return pl.pallas_call(
        route,
        name="route",
        out_shape=(
            jax.ShapeDtypeStruct((4 * CH * ROWS, LON), jnp.float32),
            jax.ShapeDtypeStruct((2, 2, 4 * CH, LON), jnp.float32),
            jax.ShapeDtypeStruct((2, ROWS, LON), jnp.int32),
            jax.ShapeDtypeStruct((1,), jnp.int32),
        ),
        in_specs=[hbm, hbm, smem, vmem],
        out_specs=(vmem, vmem, vmem, smem),
        scratch_shapes=scratch,
        compiler_params=pltpu.CompilerParams(
            collective_id=0, has_side_effects=True, vmem_limit_bytes=48 << 20
        ),
    )(states, pert, parents, mask)


INNER = CH * ROWS
MIDDLE = INNER + 2 * WIN
OUTER = INNER + 4 * WIN


def place(i, off):
    q = i - INNER
    window = (q >= WIN).astype(jnp.int32) + (q >= 2 * WIN) + (q >= 3 * WIN)
    inside = i < INNER
    ch = jnp.where(inside, i >> 3, q - window * WIN - off)
    outer_row = jnp.where(window == 0, -1, jnp.where(window == 1, 8, jnp.where(window == 2, -2, 9)))
    return ch, jnp.where(inside, i & 7, outer_row)


def stencil(coupling, diffusivity, rows, cols, off):
    high = functools.partial(jnp.dot, preferred_element_type=jnp.float32, precision=lax.Precision.HIGHEST)
    ch_a, _ = place(lax.broadcasted_iota(jnp.int32, (rows, CH), 0), off)
    pick_a = (ch_a == lax.broadcasted_iota(jnp.int32, (rows, CH), 1)).astype(jnp.float32)
    ch_b, _ = place(lax.broadcasted_iota(jnp.int32, (CH, cols), 1), off)
    pick_b = (ch_b == lax.broadcasted_iota(jnp.int32, (CH, cols), 0)).astype(jnp.float32)
    full = high(high(pick_a, coupling), pick_b)
    d = jnp.sum(pick_a * diffusivity, axis=1, keepdims=True)
    shape = (rows, cols)
    ci, ri = place(lax.broadcasted_iota(jnp.int32, shape, 0), off)
    cj, rj = place(lax.broadcasted_iota(jnp.int32, shape, 1), off)
    real = (ci >= 0) & (ci < CH) & (cj >= 0) & (cj < CH)
    gap = ri - rj
    vertical = jnp.where(gap == 0, -4.0, jnp.where((gap == 1) | (gap == -1), 1.0, 0.0))
    m = jnp.where(gap == 0, full, 0.0) + jnp.where(ci == cj, vertical * d, 0.0)
    return jnp.where(real, m, 0.0), d


def halves(v):
    top = v.astype(jnp.bfloat16)
    return top, (v - top.astype(jnp.float32)).astype(jnp.bfloat16)


def apply(mat, v):
    dot = functools.partial(jnp.dot, preferred_element_type=jnp.float32)
    top, low = halves(v)
    n = mat.shape[0] // 2
    both = dot(mat[...], top)
    return both[:n] + both[n:] + dot(mat[:n], low)


def sides(v):
    return pltpu.roll(v, 1, 1) + pltpu.roll(v, LON - 1, 1)


def model(res, halo, mask, mask_halo, coupling, diffusivity, out, mat1, mat2, diff, land):
    j = pl.program_id(0)
    dom = lax.axis_index("domain")
    has_low = (dom > 0).astype(jnp.float32)
    has_high = (dom < 31).astype(jnp.float32)

    @pl.when(j == 0)
    def _():
        for odd in range(2):
            m, d = stencil(coupling[...], diffusivity[...], MIDDLE, OUTER, 4 * odd)
            top, low = halves(m)
            mat1[odd, :MIDDLE] = top
            mat1[odd, MIDDLE:] = low
            diff[odd] = jnp.broadcast_to(d, (MIDDLE, 128))
            m, _ = stencil(coupling[...], diffusivity[...], INNER, MIDDLE, 4 * odd)
            top, low = halves(m)
            mat2[odd, :INNER] = top
            mat2[odd, INNER:] = low
        sea = mask[...].astype(jnp.float32)
        for c in range(CH):
            land[pl.ds(c * ROWS, ROWS)] = sea
        low = mask_halo[0, ROWS - 1 : ROWS].astype(jnp.float32) * has_low
        high = mask_halo[1, 0:1].astype(jnp.float32) * has_high
        land[pl.ds(INNER, WIN)] = jnp.broadcast_to(low, (WIN, LON))
        land[pl.ds(INNER + WIN, WIN)] = jnp.broadcast_to(high, (WIN, LON))

    odd = lax.rem(j, 2)
    start = pl.multiple_of(lax.div(j, 2) * 40 + odd * 16, 8)
    rows = pl.ds(start, WIN)
    v = jnp.concatenate(
        [
            res[0],
            halo[0, 1, rows] * has_low,
            halo[1, 0, rows] * has_high,
            halo[0, 0, rows] * has_low,
            halo[1, 1, rows] * has_high,
        ],
        axis=0,
    )
    d = diff[odd][:, :1]
    u = v[:MIDDLE]
    first = u + land[...] * (apply(mat1.at[odd], v) + d * sides(u))
    inner = first[:INNER]
    out[0] = inner + land[:INNER] * (apply(mat2.at[odd], first) + d[:INNER] * sides(inner))


def modelled(res, halo, mask, mask_halo, coupling, diffusivity):
    whole = pl.BlockSpec(memory_space=pltpu.VMEM)
    block = pl.BlockSpec((1, INNER, LON), lambda j: (j, 0, 0))
    return pl.pallas_call(
        model,
        name="model",
        grid=(4,),
        out_shape=jax.ShapeDtypeStruct((4, INNER, LON), jnp.float32),
        in_specs=[block, whole, whole, whole, whole, whole],
        out_specs=block,
        scratch_shapes=[
            pltpu.VMEM((2, 2 * MIDDLE, OUTER), jnp.bfloat16),
            pltpu.VMEM((2, 2 * INNER, MIDDLE), jnp.bfloat16),
            pltpu.VMEM((2, MIDDLE, 128), jnp.float32),
            pltpu.VMEM((MIDDLE, LON), jnp.float32),
        ],
        compiler_params=pltpu.CompilerParams(vmem_limit_bytes=48 << 20),
    )(res, halo, mask, mask_halo, coupling, diffusivity)


def with_halo(block):
    count = lax.axis_size("domain")
    forward = [(i, i + 1) for i in range(count - 1)]
    backward = [(target, source) for source, target in forward]
    low = lax.ppermute(block[:, :, -1:], "domain", forward)
    high = lax.ppermute(block[:, :, :1], "domain", backward)
    return jnp.concatenate([low, block, high], axis=2)


def advance(padded, mask_rows, diffusivity, coupling):
    center = padded[:, :, 1:-1]
    laplace = (
        padded[:, :, :-2]
        + padded[:, :, 2:]
        + jnp.roll(center, 1, 3)
        + jnp.roll(center, -1, 3)
        - 4.0 * center
    )
    coupled = jnp.einsum("cd,pdrl->pcrl", coupling, center, precision=lax.Precision.HIGHEST)
    return center + mask_rows[None, None] * (diffusivity[None, :, None, None] * laplace + coupled)


def gathered(states, parents, perturbation, sea_mask, diffusivity, coupling):
    shard_rows = lax.all_gather(states, "particle", axis=0, tiled=True)
    fields = jnp.take(shard_rows, parents, axis=0) + perturbation
    mask_rows = sea_mask.astype(jnp.float32)
    for _ in range(2):
        fields = advance(with_halo(fields), mask_rows, diffusivity, coupling)
    return fields


def on_device(states, parents, perturbation, sea_mask, diffusivity, coupling):
    res, halo, mask_halo, flag = routed(states, perturbation, parents, sea_mask)

    def usual():
        out = modelled(
            res.reshape(4, INNER, LON), halo, sea_mask, mask_halo, coupling, diffusivity[None]
        )
        return out.reshape(4, CH, ROWS, LON)

    def crowded():
        return gathered(states, parents, perturbation, sea_mask, diffusivity, coupling)

    return lax.cond(flag[0] > 0, crowded, usual)


def solution(mesh):
    in_specs = (
        P("particle", None, "domain", None),
        P("particle"),
        P("particle", None, "domain", None),
        P("domain", None),
        P(),
        P(),
    )
    out_specs = P("particle", None, "domain", None)
    return jax.shard_map(
        on_device, mesh=mesh, in_specs=in_specs, out_specs=out_specs, check_vma=False
    )
```

```python
import functools
import jax
import jax.numpy as jnp
from jax import lax
from jax.experimental import pallas as pl
from jax.experimental.pallas import tpu as pltpu
from jax.sharding import PartitionSpec as P

MESH = pl.DeviceIdType.MESH
CH, LON, ROWS = 20, 1024, 8
GROUP = 5
HALF = 16
CAP = 8
CHUNKS = 8
WIDTH = LON // CHUNKS
AHEAD = 3
LZ, LX = 2, 1
UNITS = [(k, 0, GROUP) for k in range(CHUNKS)]
N_UNITS = len(UNITS)
WIN = 24


def route(
    states, pert, parents, mask, coupling, diffusivity,
    res, halo, mask_halo, flag, mat1, mat2, diff, land, *scratch
):
    it = iter(scratch)
    take = lambda n: [next(it) for _ in range(n)]
    mine, crossing, crossed, back, got = (take(N_UNITS) for _ in range(5))
    edge = take(CHUNKS)
    (pert_v, strip, par_send, par_x, par_z, par_xs, par_zs, bits, table, listed) = (next(it) for _ in range(10))
    (s_x1, r_x1, l_x1, s_z, r_z, s_x2, r_x2, s_h, r_h, s_p, r_p, s_q, r_q, s_m, r_m, l_c) = (
        next(it) for _ in range(16)
    )
    p, dom = lax.axis_index("particle"), lax.axis_index("domain")
    x, h = lax.div(p, 2), lax.rem(p, 2)
    peer_x = [lax.rem(x + d, 4) for d in range(4)]
    peers = [(peer_x[d] * 2 + h, dom) for d in range(4)]
    partner = (x * 2 + 1 - h, dom)
    below, above = (p, lax.rem(dom + 31, 32)), (p, lax.rem(dom + 1, 32))

    def remote(src, dst, ss, rs, dev):
        return pltpu.make_async_remote_copy(
            src_ref=src, dst_ref=dst, send_sem=ss, recv_sem=rs, device_id=dev, device_id_type=MESH
        )

    lon = lambda k: pl.ds(k * WIDTH, WIDTH)
    chan = lambda g, u: pl.ds(g * GROUP + UNITS[u][1], UNITS[u][2])

    def x1(k):
        return [
            remote(
                states.at[:, chan(peer_x[d], k), :, lon(UNITS[k][0])],
                mine[k].at[pl.ds(x * 4, 4)],
                s_x1.at[k, d - 1],
                r_x1.at[k, d - 1],
                peers[d],
            )
            for d in range(1, 4)
        ]

    own = [
        pltpu.make_async_copy(
            states.at[:, chan(x, k), :, lon(UNITS[k][0])], mine[k].at[pl.ds(x * 4, 4)], l_x1.at[k]
        )
        for k in range(N_UNITS)
    ]
    pert_copy = pltpu.make_async_copy(pert, pert_v, l_c.at[0])
    pert_copy.start()
    for k in range(N_UNITS):
        own[k].start()

    lane = lax.broadcasted_iota(jnp.int32, (8, 128), 1)
    row = jnp.zeros((8, 128), jnp.int32)
    for i in range(4):
        row = jnp.where(lane == i, parents[i], row)
    par_send[...] = row
    par_x[pl.ds(x, 1)] = row[None]

    barrier = pltpu.get_barrier_semaphore()
    for dev in peers[1:] + [partner, below, above]:
        pl.semaphore_signal(barrier, inc=1, device_id=dev, device_id_type=MESH)
    pl.semaphore_wait(barrier, 6)

    sent = []

    def go(copies):
        for c in copies:
            c.start()
        sent.extend(copies)
        return copies

    par = go([remote(par_send, par_x.at[x], s_p.at[d - 1], r_p.at[d - 1], peers[d]) for d in range(1, 4)])
    first = {k: go(x1(k)) for k in range(AHEAD)}
    masks = [
        remote(mask, mask_halo.at[1], s_m.at[0], r_m.at[0], below),
        remote(mask, mask_halo.at[0], s_m.at[1], r_m.at[1], above),
    ]
    pl.when(dom > 0)(masks[0].start)
    pl.when(dom < 31)(masks[1].start)

    @pl.when(dom == 0)
    def _():
        halo[0] = jnp.zeros(halo.shape[1:], jnp.float32)
        mask_halo[0] = jnp.zeros(mask_halo.shape[1:], jnp.int32)

    @pl.when(dom == 31)
    def _():
        halo[1] = jnp.zeros(halo.shape[1:], jnp.float32)
        mask_halo[1] = jnp.zeros(mask_halo.shape[1:], jnp.int32)

    for c in par:
        c.wait_recv()
    (par2,) = go([remote(par_x, par_z, s_q.at[0], r_q.at[0], partner)])
    to_smem = pltpu.make_async_copy(par_x, par_xs, l_c.at[1])
    to_smem.start()

    def set_bit(i, b):
        bits[i] = b
        return b + b

    lax.fori_loop(0, 32, set_bit, jnp.int32(1))
    to_smem.wait()

    def union(ref):
        return lax.fori_loop(
            0, HALF, lambda i, m: m | bits[ref[lax.div(i, 4), 0, lax.rem(i, 4)]], jnp.int32(0), unroll=4
        )

    def member(l, half):
        return lax.div(l, 4) * 8 + half * 4 + lax.rem(l, 4)

    for odd in range(2):
        build(coupling[...], diffusivity[...], odd, mat1, mat2, diff)
    wanted_here = union(par_xs)

    def arrivals(l, count):
        here, there = member(l, h), member(l, 1 - h)
        table[here] = l
        table[there] = HALF + jnp.minimum(count, CAP - 1)
        return count + (lax.shift_right_logical(wanted_here, there) & 1)

    zero = jnp.int32(0)
    n_in = lax.fori_loop(0, HALF, arrivals, zero, unroll=4)
    par2.wait_recv()
    to_smem2 = pltpu.make_async_copy(par_z, par_zs, l_c.at[2])
    to_smem2.start()
    to_smem2.wait()
    wanted_there = union(par_zs)

    def departures(l, carry):
        count, out = carry
        bit = lax.shift_right_logical(wanted_there, member(l, h)) & 1
        out = tuple(
            jnp.where((bit == 1) & (count == c), l, old) for c, old in enumerate(out)
        )
        return count + bit, out

    n_out, out = lax.fori_loop(0, HALF, departures, (zero, (zero,) * CAP), unroll=4)
    for c in range(CAP):
        listed[c] = out[c]
    flag[0] = jnp.where((n_out > CAP) | (n_in > CAP), 1, 0).astype(jnp.int32)

    def wait_rows(copies):
        down, up = copies
        pl.when(dom < 31)(down.wait_recv)
        pl.when(dom > 0)(up.wait_recv)

    res4 = res.reshape(4, CH, ROWS, LON)
    strip4 = strip.reshape(4, CH, ROWS, WIDTH)
    z, second, halos = {}, {}, {}
    for t in range(N_UNITS + LZ + LX):
        if t < N_UNITS:
            k = t
            own[k].wait()
            for c in first[k]:
                c.wait_recv()

            def stage_z(c, carry, k=k):
                crossing[k][c] = mine[k][listed[c]]
                return carry

            lax.fori_loop(0, CAP, stage_z, 0)
            z[k] = go([remote(crossing[k], crossed[k], s_z.at[k], r_z.at[k], partner)])
            if k + AHEAD < N_UNITS:
                first[k + AHEAD] = go(x1(k + AHEAD))
        if t == 2:
            wait_rows(masks)
            sea = mask[...].astype(jnp.float32)
            for c in range(CH):
                land[pl.ds(c * ROWS, ROWS)] = sea
            low = mask_halo[0, ROWS - 1 : ROWS].astype(jnp.float32)
            high = mask_halo[1, 0:1].astype(jnp.float32)
            land[pl.ds(INNER, WIN)] = jnp.broadcast_to(low, (WIN, LON))
            land[pl.ds(INNER + WIN, WIN)] = jnp.broadcast_to(high, (WIN, LON))
        if LZ <= t < N_UNITS + LZ:
            k = t - LZ
            z[k][0].wait_recv()
            second[k] = []
            for d in (1, 2, 3, 0):

                def stage_x(j, carry, k=k, d=d):
                    s = table[par_xs[peer_x[d], 0, j]]
                    far = s >= HALF
                    a = mine[k][jnp.where(far, 0, s)]
                    b = crossed[k][jnp.where(far, s - HALF, 0)]
                    v = jnp.where(far, b, a)
                    if d == 0:
                        got[k][x, j] = v
                    else:
                        back[k][d - 1, j] = v
                    return carry

                lax.fori_loop(0, 4, stage_x, 0)
                if d:
                    second[k] += go(
                        [
                            remote(
                                back[k].at[d - 1],
                                got[k].at[x],
                                s_x2.at[k, d - 1],
                                r_x2.at[k, d - 1],
                                peers[d],
                            )
                        ]
                    )
        if t >= LZ + LX:
            k = t - LZ - LX
            if k == 0:
                pert_copy.wait()
            for c in second[k]:
                c.wait_recv()
            u, (k, _, _) = k, UNITS[k]
            for g in range(4):
                new = got[u][g] + pert_v[:, chan(g, u), :, lon(k)]
                res4[:, chan(g, u), :, lon(k)] = new
                strip4[:, chan(g, u)] = new
            if u + 1 < N_UNITS and UNITS[u + 1][0] == k:
                continue
            for i, r in enumerate((0, 1, 6, 7)):
                edge[k][i // 2, i % 2] = strip[pl.ds(r, 4 * CH, stride=ROWS)]
            halos[k] = [
                remote(edge[k].at[0], halo.at[1, :, :, lon(k)], s_h.at[k, 0], r_h.at[k, 0], below),
                remote(edge[k].at[1], halo.at[0, :, :, lon(k)], s_h.at[k, 1], r_h.at[k, 1], above),
            ]
            pl.when(dom > 0)(halos[k][0].start)
            pl.when(dom < 31)(halos[k][1].start)
    for k in range(CHUNKS):
        wait_rows(halos[k])
    for c in sent:
        c.wait_send()
    for down, up in [masks] + [halos[k] for k in range(CHUNKS)]:
        pl.when(dom > 0)(down.wait_send)
        pl.when(dom < 31)(up.wait_send)


def routed(states, pert, parents, mask, coupling, diffusivity):
    dma = pltpu.SemaphoreType.DMA
    vm = lambda *s: pltpu.VMEM(s, jnp.float32)
    scratch = []
    for lead in ((HALF,), (CAP,), (CAP,), (3, 4), (4, 4)):
        scratch += [vm(*lead, unit[2], ROWS, WIDTH) for unit in UNITS]
    scratch += [vm(2, 2, 4 * CH, WIDTH)] * CHUNKS
    scratch += [
        vm(4, CH, ROWS, LON),
        vm(4 * CH * ROWS, WIDTH),
        pltpu.VMEM((8, 128), jnp.int32),
        pltpu.VMEM((4, 8, 128), jnp.int32),
        pltpu.VMEM((4, 8, 128), jnp.int32),
        pltpu.SMEM((4, 8, 128), jnp.int32),
        pltpu.SMEM((4, 8, 128), jnp.int32),
        pltpu.SMEM((32,), jnp.int32),
        pltpu.SMEM((32,), jnp.int32),
        pltpu.SMEM((CAP,), jnp.int32),
    ]
    three, two, one = dma((N_UNITS, 3)), dma((CHUNKS, 2)), dma((N_UNITS,))
    scratch += [three, three, one, one, one, three, three, two, two, dma((3,)), dma((3,)), dma((1,)), dma((1,)), dma((2,)), dma((2,)), dma((3,))]
    vmem = pl.BlockSpec(memory_space=pltpu.VMEM)
    smem = pl.BlockSpec(memory_space=pltpu.SMEM)
    hbm = pl.BlockSpec(memory_space=pl.ANY)
    return pl.pallas_call(
        route,
        name="route",
        out_shape=(
            jax.ShapeDtypeStruct((4 * CH * ROWS, LON), jnp.float32),
            jax.ShapeDtypeStruct((2, 2, 4 * CH, LON), jnp.float32),
            jax.ShapeDtypeStruct((2, ROWS, LON), jnp.int32),
            jax.ShapeDtypeStruct((1,), jnp.int32),
            jax.ShapeDtypeStruct((2, 2 * MIDDLE, OUTER), jnp.bfloat16),
            jax.ShapeDtypeStruct((2, 2 * INNER, MIDDLE), jnp.bfloat16),
            jax.ShapeDtypeStruct((2, MIDDLE, 128), jnp.float32),
            jax.ShapeDtypeStruct((MIDDLE, LON), jnp.float32),
        ),
        in_specs=[hbm, hbm, smem, vmem, vmem, vmem],
        out_specs=(vmem, vmem, vmem, smem, vmem, vmem, vmem, vmem),
        scratch_shapes=scratch,
        compiler_params=pltpu.CompilerParams(
            collective_id=0, has_side_effects=True, vmem_limit_bytes=48 << 20
        ),
    )(states, pert, parents, mask, coupling, diffusivity)


INNER = CH * ROWS
MIDDLE = INNER + 2 * WIN
OUTER = INNER + 4 * WIN


def place(i, off):
    q = i - INNER
    window = (q >= WIN).astype(jnp.int32) + (q >= 2 * WIN) + (q >= 3 * WIN)
    inside = i < INNER
    ch = jnp.where(inside, i >> 3, q - window * WIN - off)
    outer_row = jnp.where(window == 0, -1, jnp.where(window == 1, 8, jnp.where(window == 2, -2, 9)))
    return ch, jnp.where(inside, i & 7, outer_row)


def stencil(coupling, diffusivity, rows, cols, off):
    high = functools.partial(jnp.dot, preferred_element_type=jnp.float32, precision=lax.Precision.HIGHEST)
    ch_a, _ = place(lax.broadcasted_iota(jnp.int32, (rows, CH), 0), off)
    pick_a = (ch_a == lax.broadcasted_iota(jnp.int32, (rows, CH), 1)).astype(jnp.float32)
    ch_b, _ = place(lax.broadcasted_iota(jnp.int32, (CH, cols), 1), off)
    pick_b = (ch_b == lax.broadcasted_iota(jnp.int32, (CH, cols), 0)).astype(jnp.float32)
    full = high(high(pick_a, coupling), pick_b)
    d = jnp.sum(pick_a * diffusivity, axis=1, keepdims=True)
    shape = (rows, cols)
    ci, ri = place(lax.broadcasted_iota(jnp.int32, shape, 0), off)
    cj, rj = place(lax.broadcasted_iota(jnp.int32, shape, 1), off)
    real = (ci >= 0) & (ci < CH) & (cj >= 0) & (cj < CH)
    gap = ri - rj
    vertical = jnp.where(gap == 0, -4.0, jnp.where((gap == 1) | (gap == -1), 1.0, 0.0))
    m = jnp.where(gap == 0, full, 0.0) + jnp.where(ci == cj, vertical * d, 0.0)
    return jnp.where(real, m, 0.0), d


def halves(v):
    top = v.astype(jnp.bfloat16)
    return top, (v - top.astype(jnp.float32)).astype(jnp.bfloat16)


def apply(mat, v):
    dot = functools.partial(jnp.dot, preferred_element_type=jnp.float32)
    top, low = halves(v)
    n = mat.shape[0] // 2
    both = dot(mat[...], top)
    return both[:n] + both[n:] + dot(mat[:n], low)


def build(coupling, diffusivity, odd, mat1, mat2, diff):
    m, d = stencil(coupling, diffusivity, MIDDLE, OUTER, 4 * odd)
    top, low = halves(m)
    mat1[odd, :MIDDLE] = top
    mat1[odd, MIDDLE:] = low
    diff[odd] = jnp.broadcast_to(d, (MIDDLE, 128))
    m, _ = stencil(coupling, diffusivity, INNER, MIDDLE, 4 * odd)
    top, low = halves(m)
    mat2[odd, :INNER] = top
    mat2[odd, INNER:] = low


def sides(v):
    return pltpu.roll(v, 1, 1) + pltpu.roll(v, LON - 1, 1)


def model(res, halo, mat1, mat2, diff, land, out):
    j = pl.program_id(0)

    odd = lax.rem(j, 2)
    start = pl.multiple_of(lax.div(j, 2) * 40 + odd * 16, 8)
    rows = pl.ds(start, WIN)
    v = jnp.concatenate(
        [
            res[0],
            halo[0, 1, rows],
            halo[1, 0, rows],
            halo[0, 0, rows],
            halo[1, 1, rows],
        ],
        axis=0,
    )
    d = diff[odd][:, :1]
    u = v[:MIDDLE]
    first = u + land[...] * (apply(mat1.at[odd], v) + d * sides(u))
    inner = first[:INNER]
    out[0] = inner + land[:INNER] * (apply(mat2.at[odd], first) + d[:INNER] * sides(inner))


def modelled(res, halo, mat1, mat2, diff, land):
    whole = pl.BlockSpec(memory_space=pltpu.VMEM)
    block = pl.BlockSpec((1, INNER, LON), lambda j: (j, 0, 0))
    return pl.pallas_call(
        model,
        name="model",
        grid=(4,),
        out_shape=pltpu.HBM((4, INNER, LON), jnp.float32),
        in_specs=[block, whole, whole, whole, whole, whole],
        out_specs=block,
        compiler_params=pltpu.CompilerParams(vmem_limit_bytes=48 << 20),
    )(res, halo, mat1, mat2, diff, land)


def with_halo(block):
    count = lax.axis_size("domain")
    forward = [(i, i + 1) for i in range(count - 1)]
    backward = [(target, source) for source, target in forward]
    low = lax.ppermute(block[:, :, -1:], "domain", forward)
    high = lax.ppermute(block[:, :, :1], "domain", backward)
    return jnp.concatenate([low, block, high], axis=2)


def advance(padded, mask_rows, diffusivity, coupling):
    center = padded[:, :, 1:-1]
    laplace = (
        padded[:, :, :-2]
        + padded[:, :, 2:]
        + jnp.roll(center, 1, 3)
        + jnp.roll(center, -1, 3)
        - 4.0 * center
    )
    coupled = jnp.einsum("cd,pdrl->pcrl", coupling, center, precision=lax.Precision.HIGHEST)
    return center + mask_rows[None, None] * (diffusivity[None, :, None, None] * laplace + coupled)


def gathered(states, parents, perturbation, sea_mask, diffusivity, coupling):
    shard_rows = lax.all_gather(states, "particle", axis=0, tiled=True)
    fields = jnp.take(shard_rows, parents, axis=0) + perturbation
    mask_rows = sea_mask.astype(jnp.float32)
    for _ in range(2):
        fields = advance(with_halo(fields), mask_rows, diffusivity, coupling)
    return fields


def on_device(states, parents, perturbation, sea_mask, diffusivity, coupling):
    res, halo, _, flag, *fixed = routed(
        states, perturbation, parents, sea_mask, coupling, diffusivity[None]
    )

    def usual():
        return modelled(res.reshape(4, INNER, LON), halo, *fixed).reshape(4, CH, ROWS, LON)

    def crowded():
        return gathered(states, parents, perturbation, sea_mask, diffusivity, coupling)

    return lax.cond(flag[0] > 0, crowded, usual)


def solution(mesh):
    in_specs = (
        P("particle", None, "domain", None),
        P("particle"),
        P("particle", None, "domain", None),
        P("domain", None),
        P(),
        P(),
    )
    out_specs = P("particle", None, "domain", None)
    return jax.shard_map(
        on_device, mesh=mesh, in_specs=in_specs, out_specs=out_specs, check_vma=False
    )
```

```python
import functools
import jax
import jax.numpy as jnp
from jax import lax
from jax.experimental import pallas as pl
from jax.experimental.pallas import tpu as pltpu
from jax.sharding import PartitionSpec as P

MESH = pl.DeviceIdType.MESH
CH, LON, ROWS = 20, 1024, 8
GROUP = 5
HALF = 16
CAPS = (5, 6, 7, 8, 16)
CHUNKS = 8
WIDTH = LON // CHUNKS
EARLY = 2
AHEAD = 3
LZ, LX = 2, 1
WIN = 24


def remote(src, dst, ss, rs, dev):
    return pltpu.make_async_remote_copy(
        src_ref=src, dst_ref=dst, send_sem=ss, recv_sem=rs, device_id=dev, device_id_type=MESH
    )


def lon(k):
    return pl.ds(k * WIDTH, WIDTH)


def chan(g):
    return pl.ds(g * GROUP, GROUP)


def where_am_i():
    p, dom = lax.axis_index("particle"), lax.axis_index("domain")
    x, h = lax.div(p, 2), lax.rem(p, 2)
    peer_x = [lax.rem(x + d, 4) for d in range(4)]
    peers = [(peer_x[d] * 2 + h, dom) for d in range(4)]
    partner = (x * 2 + 1 - h, dom)
    below, above = (p, lax.rem(dom + 31, 32)), (p, lax.rem(dom + 1, 32))
    return dom, x, h, peer_x, peers, partner, below, above


def meet(devices):
    barrier = pltpu.get_barrier_semaphore()
    for dev in devices:
        pl.semaphore_signal(barrier, inc=1, device_id=dev, device_id_type=MESH)
    pl.semaphore_wait(barrier, len(devices))


def spread(states, mine, k, x, peer_x, peers, ss, rs):
    return [
        remote(
            states.at[:, chan(peer_x[d]), :, lon(k)],
            mine[k].at[pl.ds(x * 4, 4)],
            ss.at[k, d - 1],
            rs.at[k, d - 1],
            peers[d],
        )
        for d in range(1, 4)
    ]


def keep(states, mine, k, x, sem):
    return pltpu.make_async_copy(
        states.at[:, chan(x), :, lon(k)], mine[k].at[pl.ds(x * 4, 4)], sem.at[k]
    )


def wait_rows(dom, copies):
    down, up = copies
    pl.when(dom < 31)(down.wait_recv)
    pl.when(dom > 0)(up.wait_recv)


def wait_rows_sent(dom, copies):
    down, up = copies
    pl.when(dom > 0)(down.wait_send)
    pl.when(dom < 31)(up.wait_send)


def plan(states, parents, *refs):
    mine, refs = refs[:EARLY], refs[EARLY:]
    sel, listed, branch, *refs = refs
    par_send, par_x, par_z, par_xs, par_zs, bits, table, *sems = refs
    s_x1, r_x1, l_x1, s_p, r_p, s_q, r_q, l_c = sems
    _, x, h, peer_x, peers, partner, _, _ = where_am_i()
    own = [keep(states, mine, k, x, l_x1) for k in range(EARLY)]
    for c in own:
        c.start()
    lane = lax.broadcasted_iota(jnp.int32, (8, 128), 1)
    row = jnp.zeros((8, 128), jnp.int32)
    for i in range(4):
        row = jnp.where(lane == i, parents[i], row)
    par_send[...] = row
    par_x[pl.ds(x, 1)] = row[None]
    meet(peers[1:] + [partner])

    par = [remote(par_send, par_x.at[x], s_p.at[d - 1], r_p.at[d - 1], peers[d]) for d in range(1, 4)]
    first = sum((spread(states, mine, k, x, peer_x, peers, s_x1, r_x1) for k in range(EARLY)), [])
    for c in par + first:
        c.start()
    for c in par:
        c.wait_recv()
    par2 = remote(par_x, par_z, s_q.at[0], r_q.at[0], partner)
    par2.start()
    to_smem = pltpu.make_async_copy(par_x, par_xs, l_c.at[0])
    to_smem.start()

    def set_bit(i, b):
        bits[i] = b
        return b + b

    lax.fori_loop(0, 32, set_bit, jnp.int32(1))
    to_smem.wait()

    def union(ref):
        return lax.fori_loop(
            0, HALF, lambda i, m: m | bits[ref[lax.div(i, 4), 0, lax.rem(i, 4)]], jnp.int32(0), unroll=4
        )

    def member(l, half):
        return lax.div(l, 4) * 8 + half * 4 + lax.rem(l, 4)

    wanted_here = union(par_xs)

    def arrivals(l, count):
        here, there = member(l, h), member(l, 1 - h)
        table[here] = l
        table[there] = HALF + jnp.minimum(count, HALF - 1)
        return count + (lax.shift_right_logical(wanted_here, there) & 1)

    zero = jnp.int32(0)
    n_in = lax.fori_loop(0, HALF, arrivals, zero, unroll=4)

    def choose(i, carry):
        sel[i] = table[par_xs[lax.div(i, 4), 0, lax.rem(i, 4)]]
        return carry

    lax.fori_loop(0, HALF, choose, 0, unroll=4)
    par2.wait_recv()
    to_smem2 = pltpu.make_async_copy(par_z, par_zs, l_c.at[1])
    to_smem2.start()
    to_smem2.wait()
    wanted_there = union(par_zs)

    def departures(l, carry):
        count, out = carry
        bit = lax.shift_right_logical(wanted_there, member(l, h)) & 1
        out = tuple(
            jnp.where((bit == 1) & (count == c), l, old) for c, old in enumerate(out)
        )
        return count + bit, out

    n_out, out = lax.fori_loop(0, HALF, departures, (zero, (zero,) * HALF), unroll=4)
    for c in range(HALF):
        listed[c] = out[c]
    most = jnp.maximum(n_out, n_in)
    branch[0] = sum((most > cap).astype(jnp.int32) for cap in CAPS[:-1])
    for c in own:
        c.wait()
    for c in par + first:
        c.wait_send()
    for c in first:
        c.wait_recv()
    par2.wait_send()


def planned(states, parents):
    dma = pltpu.SemaphoreType.DMA
    vmem = pl.BlockSpec(memory_space=pltpu.VMEM)
    smem = pl.BlockSpec(memory_space=pltpu.SMEM)
    hbm = pl.BlockSpec(memory_space=pl.ANY)
    shape = jax.ShapeDtypeStruct
    ints = lambda *s: pltpu.SMEM(s, jnp.int32)
    return pl.pallas_call(
        plan,
        name="plan",
        out_shape=[shape((HALF, GROUP, ROWS, WIDTH), jnp.float32)] * EARLY
        + [
            shape((HALF,), jnp.int32),
            shape((HALF,), jnp.int32),
            shape((1,), jnp.int32),
        ],
        in_specs=[hbm, smem],
        out_specs=[vmem] * EARLY + [smem] * 3,
        scratch_shapes=[
            pltpu.VMEM((8, 128), jnp.int32),
            pltpu.VMEM((4, 8, 128), jnp.int32),
            pltpu.VMEM((4, 8, 128), jnp.int32),
            ints(4, 8, 128),
            ints(4, 8, 128),
            ints(32),
            ints(32),
            dma((EARLY, 3)),
            dma((EARLY, 3)),
            dma((EARLY,)),
            dma((3,)),
            dma((3,)),
            dma((1,)),
            dma((1,)),
            dma((2,)),
        ],
        compiler_params=pltpu.CompilerParams(
            collective_id=0, has_side_effects=True, vmem_limit_bytes=48 << 20
        ),
    )(states, parents)


def route(cap, states, pert, sel, listed, mask, coupling, diffusivity, *refs):
    mine, refs = refs[:EARLY], refs[EARLY:]
    res, halo, mat1, mat2, diff, land, *refs = refs
    it = iter(refs)
    take = lambda n: [next(it) for _ in range(n)]
    mine = list(mine) + take(CHUNKS - EARLY)
    crossing, crossed, back, got, edge = (take(CHUNKS) for _ in range(5))
    pert_v, strip, mask_halo = take(3)
    s_x1, r_x1, l_x1, s_z, r_z, s_x2, r_x2, s_h, r_h, s_m, r_m, l_c = it
    dom, x, h, peer_x, peers, partner, below, above = where_am_i()
    own = {k: keep(states, mine, k, x, l_x1) for k in range(EARLY, CHUNKS)}
    for c in own.values():
        c.start()
    pert_copy = pltpu.make_async_copy(pert, pert_v, l_c.at[0])
    pert_copy.start()

    @pl.when(dom == 0)
    def _():
        halo[0] = jnp.zeros(halo.shape[1:], jnp.float32)
        mask_halo[0] = jnp.zeros(mask_halo.shape[1:], jnp.int32)

    @pl.when(dom == 31)
    def _():
        halo[1] = jnp.zeros(halo.shape[1:], jnp.float32)
        mask_halo[1] = jnp.zeros(mask_halo.shape[1:], jnp.int32)

    masks = [
        remote(mask, mask_halo.at[1], s_m.at[0], r_m.at[0], below),
        remote(mask, mask_halo.at[0], s_m.at[1], r_m.at[1], above),
    ]
    sent = []

    def go(copies):
        for c in copies:
            c.start()
        sent.extend(copies)
        return copies

    def stage_z(k):
        def body(c, carry):
            crossing[k][c] = mine[k][listed[c]]
            return carry

        lax.fori_loop(0, cap, body, 0)

    stage_z(0)
    meet(peers[1:] + [partner, below, above])
    x1 = lambda k: go(spread(states, mine, k, x, peer_x, peers, s_x1, r_x1))
    first = {}
    res4 = res.reshape(4, CH, ROWS, LON)
    strip4 = strip.reshape(4, CH, ROWS, WIDTH)
    z, second, halos = {}, {}, {}
    for t in range(CHUNKS + LZ + LX):
        if t < CHUNKS:
            k = t
            if k >= EARLY:
                own[k].wait()
                for c in first[k]:
                    c.wait_recv()
            if k:
                stage_z(k)
            z[k] = go([remote(crossing[k], crossed[k], s_z.at[k], r_z.at[k], partner)])
            for j in range(EARLY, AHEAD + 1) if k == 0 else [k + AHEAD]:
                if j < CHUNKS:
                    first[j] = x1(j)
        if t == 0:
            pl.when(dom > 0)(masks[0].start)
            pl.when(dom < 31)(masks[1].start)
        if t == 1:
            for odd in range(2):
                build(coupling[...], diffusivity[...], odd, mat1, mat2, diff)
            wait_rows(dom, masks)
            sea = mask[...].astype(jnp.float32)
            for c in range(CH):
                land[pl.ds(c * ROWS, ROWS)] = sea
            low = mask_halo[0, ROWS - 1 : ROWS].astype(jnp.float32)
            high = mask_halo[1, 0:1].astype(jnp.float32)
            land[pl.ds(INNER, WIN)] = jnp.broadcast_to(low, (WIN, LON))
            land[pl.ds(INNER + WIN, WIN)] = jnp.broadcast_to(high, (WIN, LON))
        if LZ <= t < CHUNKS + LZ:
            k = t - LZ
            z[k][0].wait_recv()
            second[k] = []
            for d in (1, 2, 3, 0):

                def stage_x(j, carry, k=k, d=d):
                    s = sel[peer_x[d] * 4 + j]
                    far = s >= HALF
                    a = mine[k][jnp.where(far, 0, s)]
                    b = crossed[k][jnp.where(far, s - HALF, 0)]
                    v = jnp.where(far, b, a)
                    if d == 0:
                        got[k][x, j] = v
                    else:
                        back[k][d - 1, j] = v
                    return carry

                lax.fori_loop(0, 4, stage_x, 0)
                if d:
                    second[k] += go(
                        [
                            remote(
                                back[k].at[d - 1],
                                got[k].at[x],
                                s_x2.at[k, d - 1],
                                r_x2.at[k, d - 1],
                                peers[d],
                            )
                        ]
                    )
        if t >= LZ + LX:
            k = t - LZ - LX
            if k == 0:
                pert_copy.wait()
            for c in second[k]:
                c.wait_recv()
            for g in range(4):
                new = got[k][g] + pert_v[:, chan(g), :, lon(k)]
                res4[:, chan(g), :, lon(k)] = new
                strip4[:, chan(g)] = new
            for i, r in enumerate((0, 1, 6, 7)):
                edge[k][i // 2, i % 2] = strip[pl.ds(r, 4 * CH, stride=ROWS)]
            halos[k] = [
                remote(edge[k].at[0], halo.at[1, :, :, lon(k)], s_h.at[k, 0], r_h.at[k, 0], below),
                remote(edge[k].at[1], halo.at[0, :, :, lon(k)], s_h.at[k, 1], r_h.at[k, 1], above),
            ]
            pl.when(dom > 0)(halos[k][0].start)
            pl.when(dom < 31)(halos[k][1].start)
    for k in range(CHUNKS):
        wait_rows(dom, halos[k])
    for c in sent:
        c.wait_send()
    for copies in [masks] + [halos[k] for k in range(CHUNKS)]:
        wait_rows_sent(dom, copies)


def routed(cap, states, pert, sel, listed, mask, coupling, diffusivity, *mine):
    dma = pltpu.SemaphoreType.DMA
    vm = lambda *s: pltpu.VMEM(s, jnp.float32)
    vmem = pl.BlockSpec(memory_space=pltpu.VMEM)
    smem = pl.BlockSpec(memory_space=pltpu.SMEM)
    hbm = pl.BlockSpec(memory_space=pl.ANY)
    scratch = [vm(HALF, GROUP, ROWS, WIDTH)] * (CHUNKS - EARLY)
    for lead in ((cap,), (cap,), (3, 4), (4, 4)):
        scratch += [vm(*lead, GROUP, ROWS, WIDTH)] * CHUNKS
    scratch += [vm(2, 2, 4 * CH, WIDTH)] * CHUNKS
    scratch += [vm(4, CH, ROWS, LON), vm(4 * CH * ROWS, WIDTH)]
    scratch += [pltpu.VMEM((2, ROWS, LON), jnp.int32)]
    three, two, one = dma((CHUNKS, 3)), dma((CHUNKS, 2)), dma((CHUNKS,))
    scratch += [three, three, one, one, one, three, three, two, two, dma((2,)), dma((2,)), dma((1,))]
    return pl.pallas_call(
        functools.partial(route, cap),
        name=f"route{cap}",
        out_shape=(
            jax.ShapeDtypeStruct((4 * CH * ROWS, LON), jnp.float32),
            jax.ShapeDtypeStruct((2, 2, 4 * CH, LON), jnp.float32),
            jax.ShapeDtypeStruct((2, 2 * MIDDLE, OUTER), jnp.bfloat16),
            jax.ShapeDtypeStruct((2, 2 * INNER, MIDDLE), jnp.bfloat16),
            jax.ShapeDtypeStruct((2, MIDDLE, 128), jnp.float32),
            jax.ShapeDtypeStruct((MIDDLE, LON), jnp.float32),
        ),
        in_specs=[hbm, hbm, smem, smem] + [vmem] * (3 + EARLY),
        out_specs=(vmem,) * 6,
        scratch_shapes=scratch,
        compiler_params=pltpu.CompilerParams(
            collective_id=1 + CAPS.index(cap), has_side_effects=True, vmem_limit_bytes=48 << 20
        ),
    )(states, pert, sel, listed, mask, coupling, diffusivity, *mine)


INNER = CH * ROWS
MIDDLE = INNER + 2 * WIN
OUTER = INNER + 4 * WIN


def place(i, off):
    q = i - INNER
    window = (q >= WIN).astype(jnp.int32) + (q >= 2 * WIN) + (q >= 3 * WIN)
    inside = i < INNER
    ch = jnp.where(inside, i >> 3, q - window * WIN - off)
    outer_row = jnp.where(window == 0, -1, jnp.where(window == 1, 8, jnp.where(window == 2, -2, 9)))
    return ch, jnp.where(inside, i & 7, outer_row)


def stencil(coupling, diffusivity, rows, cols, off):
    high = functools.partial(jnp.dot, preferred_element_type=jnp.float32, precision=lax.Precision.HIGHEST)
    ch_a, _ = place(lax.broadcasted_iota(jnp.int32, (rows, CH), 0), off)
    pick_a = (ch_a == lax.broadcasted_iota(jnp.int32, (rows, CH), 1)).astype(jnp.float32)
    ch_b, _ = place(lax.broadcasted_iota(jnp.int32, (CH, cols), 1), off)
    pick_b = (ch_b == lax.broadcasted_iota(jnp.int32, (CH, cols), 0)).astype(jnp.float32)
    full = high(high(pick_a, coupling), pick_b)
    d = jnp.sum(pick_a * diffusivity, axis=1, keepdims=True)
    shape = (rows, cols)
    ci, ri = place(lax.broadcasted_iota(jnp.int32, shape, 0), off)
    cj, rj = place(lax.broadcasted_iota(jnp.int32, shape, 1), off)
    real = (ci >= 0) & (ci < CH) & (cj >= 0) & (cj < CH)
    gap = ri - rj
    vertical = jnp.where(gap == 0, -4.0, jnp.where((gap == 1) | (gap == -1), 1.0, 0.0))
    m = jnp.where(gap == 0, full, 0.0) + jnp.where(ci == cj, vertical * d, 0.0)
    return jnp.where(real, m, 0.0), d


def halves(v):
    top = v.astype(jnp.bfloat16)
    return top, (v - top.astype(jnp.float32)).astype(jnp.bfloat16)


def apply(mat, v):
    dot = functools.partial(jnp.dot, preferred_element_type=jnp.float32)
    top, low = halves(v)
    n = mat.shape[0] // 2
    both = dot(mat[...], top)
    return both[:n] + both[n:] + dot(mat[:n], low)


def build(coupling, diffusivity, odd, mat1, mat2, diff):
    m, d = stencil(coupling, diffusivity, MIDDLE, OUTER, 4 * odd)
    top, low = halves(m)
    mat1[odd, :MIDDLE] = top
    mat1[odd, MIDDLE:] = low
    diff[odd] = jnp.broadcast_to(d, (MIDDLE, 128))
    m, _ = stencil(coupling, diffusivity, INNER, MIDDLE, 4 * odd)
    top, low = halves(m)
    mat2[odd, :INNER] = top
    mat2[odd, INNER:] = low


def sides(v):
    return pltpu.roll(v, 1, 1) + pltpu.roll(v, LON - 1, 1)


def model(res, halo, mat1, mat2, diff, land, out):
    j = pl.program_id(0)

    odd = lax.rem(j, 2)
    start = pl.multiple_of(lax.div(j, 2) * 40 + odd * 16, 8)
    rows = pl.ds(start, WIN)
    v = jnp.concatenate(
        [
            res[0],
            halo[0, 1, rows],
            halo[1, 0, rows],
            halo[0, 0, rows],
            halo[1, 1, rows],
        ],
        axis=0,
    )
    d = diff[odd][:, :1]
    u = v[:MIDDLE]
    first = u + land[...] * (apply(mat1.at[odd], v) + d * sides(u))
    inner = first[:INNER]
    out[0] = inner + land[:INNER] * (apply(mat2.at[odd], first) + d[:INNER] * sides(inner))


def modelled(res, halo, mat1, mat2, diff, land):
    whole = pl.BlockSpec(memory_space=pltpu.VMEM)
    block = pl.BlockSpec((1, INNER, LON), lambda j: (j, 0, 0))
    return pl.pallas_call(
        model,
        name="model",
        grid=(4,),
        out_shape=pltpu.HBM((4, INNER, LON), jnp.float32),
        in_specs=[block, whole, whole, whole, whole, whole],
        out_specs=block,
        compiler_params=pltpu.CompilerParams(vmem_limit_bytes=48 << 20),
    )(res, halo, mat1, mat2, diff, land)


def on_device(states, parents, perturbation, sea_mask, diffusivity, coupling):
    *mine, sel, listed, branch = planned(states, parents)
    res, *others = lax.switch(
        branch[0],
        [functools.partial(routed, cap) for cap in CAPS],
        states,
        perturbation,
        sel,
        listed,
        sea_mask,
        coupling,
        diffusivity[None],
        *mine,
    )
    return modelled(res.reshape(4, INNER, LON), *others).reshape(4, CH, ROWS, LON)


def solution(mesh):
    in_specs = (
        P("particle", None, "domain", None),
        P("particle"),
        P("particle", None, "domain", None),
        P("domain", None),
        P(),
        P(),
    )
    out_specs = P("particle", None, "domain", None)
    return jax.shard_map(
        on_device, mesh=mesh, in_specs=in_specs, out_specs=out_specs, check_vma=False
    )
```

```python
import functools
import jax
import jax.numpy as jnp
from jax import lax
from jax.experimental import pallas as pl
from jax.experimental.pallas import tpu as pltpu
from jax.sharding import PartitionSpec as P

MESH = pl.DeviceIdType.MESH
CH, LON, ROWS = 20, 1024, 8
GROUP = 5
HALF = 16
CAPS = (5, 6, 7, 8, 16)
CHUNKS = 8
WIDTH = LON // CHUNKS
EARLY = 2
AHEAD = 2
LZ, LX = 2, 2
WIN = 24


def remote(src, dst, ss, rs, dev):
    return pltpu.make_async_remote_copy(
        src_ref=src, dst_ref=dst, send_sem=ss, recv_sem=rs, device_id=dev, device_id_type=MESH
    )


def lon(k):
    return pl.ds(k * WIDTH, WIDTH)


def chan(g):
    return pl.ds(g * GROUP, GROUP)


def where_am_i():
    p, dom = lax.axis_index("particle"), lax.axis_index("domain")
    x, h = lax.div(p, 2), lax.rem(p, 2)
    peer_x = [lax.rem(x + d, 4) for d in range(4)]
    peers = [(peer_x[d] * 2 + h, dom) for d in range(4)]
    partner = (x * 2 + 1 - h, dom)
    below, above = (p, lax.rem(dom + 31, 32)), (p, lax.rem(dom + 1, 32))
    return dom, x, h, peer_x, peers, partner, below, above


def meet(devices):
    barrier = pltpu.get_barrier_semaphore()
    for dev in devices:
        pl.semaphore_signal(barrier, inc=1, device_id=dev, device_id_type=MESH)
    pl.semaphore_wait(barrier, len(devices))


def spread(states, mine, k, x, peer_x, peers, ss, rs):
    return [
        remote(
            states.at[:, chan(peer_x[d]), :, lon(k)],
            mine[k].at[pl.ds(x * 4, 4)],
            ss.at[k, d - 1],
            rs.at[k, d - 1],
            peers[d],
        )
        for d in range(1, 4)
    ]


def keep(states, mine, k, x, sem):
    return pltpu.make_async_copy(
        states.at[:, chan(x), :, lon(k)], mine[k].at[pl.ds(x * 4, 4)], sem.at[k]
    )


def wait_rows(dom, copies):
    down, up = copies
    pl.when(dom < 31)(down.wait_recv)
    pl.when(dom > 0)(up.wait_recv)


def wait_rows_sent(dom, copies):
    down, up = copies
    pl.when(dom > 0)(down.wait_send)
    pl.when(dom < 31)(up.wait_send)


def plan(states, parents, *refs):
    mine, refs = refs[:EARLY], refs[EARLY:]
    sel, listed, branch, *refs = refs
    par_send, par_x, par_z, par_xs, par_zs, bits, table, *sems = refs
    s_x1, r_x1, l_x1, s_p, r_p, s_q, r_q, l_c = sems
    _, x, h, peer_x, peers, partner, _, _ = where_am_i()
    own = [keep(states, mine, k, x, l_x1) for k in range(EARLY)]
    for c in own:
        c.start()
    lane = lax.broadcasted_iota(jnp.int32, (8, 128), 1)
    row = jnp.zeros((8, 128), jnp.int32)
    for i in range(4):
        row = jnp.where(lane == i, parents[i], row)
    par_send[...] = row
    par_x[pl.ds(x, 1)] = row[None]
    meet(peers[1:] + [partner])

    par = [remote(par_send, par_x.at[x], s_p.at[d - 1], r_p.at[d - 1], peers[d]) for d in range(1, 4)]
    first = sum((spread(states, mine, k, x, peer_x, peers, s_x1, r_x1) for k in range(EARLY)), [])
    for c in par + first:
        c.start()
    for c in par:
        c.wait_recv()
    par2 = remote(par_x, par_z, s_q.at[0], r_q.at[0], partner)
    par2.start()
    to_smem = pltpu.make_async_copy(par_x, par_xs, l_c.at[0])
    to_smem.start()

    def set_bit(i, b):
        bits[i] = b
        return b + b

    lax.fori_loop(0, 32, set_bit, jnp.int32(1))
    to_smem.wait()

    def union(ref):
        return lax.fori_loop(
            0, HALF, lambda i, m: m | bits[ref[lax.div(i, 4), 0, lax.rem(i, 4)]], jnp.int32(0), unroll=4
        )

    def member(l, half):
        return lax.div(l, 4) * 8 + half * 4 + lax.rem(l, 4)

    wanted_here = union(par_xs)

    def arrivals(l, count):
        here, there = member(l, h), member(l, 1 - h)
        table[here] = l
        table[there] = HALF + jnp.minimum(count, HALF - 1)
        return count + (lax.shift_right_logical(wanted_here, there) & 1)

    zero = jnp.int32(0)
    n_in = lax.fori_loop(0, HALF, arrivals, zero, unroll=4)

    def choose(i, carry):
        sel[i] = table[par_xs[lax.div(i, 4), 0, lax.rem(i, 4)]]
        return carry

    lax.fori_loop(0, HALF, choose, 0, unroll=4)
    par2.wait_recv()
    to_smem2 = pltpu.make_async_copy(par_z, par_zs, l_c.at[1])
    to_smem2.start()
    to_smem2.wait()
    wanted_there = union(par_zs)

    def departures(l, carry):
        count, out = carry
        bit = lax.shift_right_logical(wanted_there, member(l, h)) & 1
        out = tuple(
            jnp.where((bit == 1) & (count == c), l, old) for c, old in enumerate(out)
        )
        return count + bit, out

    n_out, out = lax.fori_loop(0, HALF, departures, (zero, (zero,) * HALF), unroll=4)
    for c in range(HALF):
        listed[c] = out[c]
    most = jnp.maximum(n_out, n_in)
    branch[0] = sum((most > cap).astype(jnp.int32) for cap in CAPS[:-1])
    for c in own:
        c.wait()
    for c in par + first:
        c.wait_send()
    for c in first:
        c.wait_recv()
    par2.wait_send()


def planned(states, parents):
    dma = pltpu.SemaphoreType.DMA
    vmem = pl.BlockSpec(memory_space=pltpu.VMEM)
    smem = pl.BlockSpec(memory_space=pltpu.SMEM)
    hbm = pl.BlockSpec(memory_space=pl.ANY)
    shape = jax.ShapeDtypeStruct
    ints = lambda *s: pltpu.SMEM(s, jnp.int32)
    return pl.pallas_call(
        plan,
        name="plan",
        out_shape=[shape((HALF, GROUP, ROWS, WIDTH), jnp.float32)] * EARLY
        + [
            shape((HALF,), jnp.int32),
            shape((HALF,), jnp.int32),
            shape((1,), jnp.int32),
        ],
        in_specs=[hbm, smem],
        out_specs=[vmem] * EARLY + [smem] * 3,
        scratch_shapes=[
            pltpu.VMEM((8, 128), jnp.int32),
            pltpu.VMEM((4, 8, 128), jnp.int32),
            pltpu.VMEM((4, 8, 128), jnp.int32),
            ints(4, 8, 128),
            ints(4, 8, 128),
            ints(32),
            ints(32),
            dma((EARLY, 3)),
            dma((EARLY, 3)),
            dma((EARLY,)),
            dma((3,)),
            dma((3,)),
            dma((1,)),
            dma((1,)),
            dma((2,)),
        ],
        compiler_params=pltpu.CompilerParams(
            collective_id=0, has_side_effects=True, vmem_limit_bytes=48 << 20
        ),
    )(states, parents)


def route(cap, states, pert, sel, listed, mask, coupling, diffusivity, *refs):
    mine, refs = refs[:EARLY], refs[EARLY:]
    res, halo, mat1, mat2, diff, land, *refs = refs
    it = iter(refs)
    take = lambda n: [next(it) for _ in range(n)]
    mine = list(mine) + take(CHUNKS - EARLY)
    crossing, crossed, back, got, edge = (take(CHUNKS) for _ in range(5))
    pert_v, strip, mask_halo = take(3)
    s_x1, r_x1, l_x1, s_z, r_z, s_x2, r_x2, s_h, r_h, s_m, r_m, l_c = it
    dom, x, h, peer_x, peers, partner, below, above = where_am_i()
    own = {k: keep(states, mine, k, x, l_x1) for k in range(EARLY, CHUNKS)}
    for c in own.values():
        c.start()
    pert_copy = pltpu.make_async_copy(pert, pert_v, l_c.at[0])
    pert_copy.start()

    @pl.when(dom == 0)
    def _():
        halo[0] = jnp.zeros(halo.shape[1:], jnp.float32)
        mask_halo[0] = jnp.zeros(mask_halo.shape[1:], jnp.int32)

    @pl.when(dom == 31)
    def _():
        halo[1] = jnp.zeros(halo.shape[1:], jnp.float32)
        mask_halo[1] = jnp.zeros(mask_halo.shape[1:], jnp.int32)

    masks = [
        remote(mask, mask_halo.at[1], s_m.at[0], r_m.at[0], below),
        remote(mask, mask_halo.at[0], s_m.at[1], r_m.at[1], above),
    ]
    sent = []

    def go(copies):
        for c in copies:
            c.start()
        sent.extend(copies)
        return copies

    def stage_z(k):
        def body(c, carry):
            crossing[k][c] = mine[k][listed[c]]
            return carry

        lax.fori_loop(0, cap, body, 0)

    stage_z(0)
    meet(peers[1:] + [partner, below, above])
    x1 = lambda k: go(spread(states, mine, k, x, peer_x, peers, s_x1, r_x1))
    first = {}
    res4 = res.reshape(4, CH, ROWS, LON)
    strip4 = strip.reshape(4, CH, ROWS, WIDTH)
    z, second, halos = {}, {}, {}
    for t in range(CHUNKS + LZ + LX):
        if t < CHUNKS:
            k = t
            if k >= EARLY:
                own[k].wait()
                for c in first[k]:
                    c.wait_recv()
            if k:
                stage_z(k)
            z[k] = go([remote(crossing[k], crossed[k], s_z.at[k], r_z.at[k], partner)])
            for j in range(EARLY, AHEAD + 1) if k == 0 else [k + AHEAD]:
                if j < CHUNKS:
                    first[j] = x1(j)
        if t == 0:
            pl.when(dom > 0)(masks[0].start)
            pl.when(dom < 31)(masks[1].start)
        if t == 1:
            for odd in range(2):
                build(coupling[...], diffusivity[...], odd, mat1, mat2, diff)
            wait_rows(dom, masks)
            sea = mask[...].astype(jnp.float32)
            for c in range(CH):
                land[pl.ds(c * ROWS, ROWS)] = sea
            low = mask_halo[0, ROWS - 1 : ROWS].astype(jnp.float32)
            high = mask_halo[1, 0:1].astype(jnp.float32)
            land[pl.ds(INNER, WIN)] = jnp.broadcast_to(low, (WIN, LON))
            land[pl.ds(INNER + WIN, WIN)] = jnp.broadcast_to(high, (WIN, LON))
        if LZ <= t < CHUNKS + LZ:
            k = t - LZ
            z[k][0].wait_recv()
            second[k] = []
            for d in (1, 2, 3, 0):

                def stage_x(j, carry, k=k, d=d):
                    s = sel[peer_x[d] * 4 + j]
                    far = s >= HALF
                    a = mine[k][jnp.where(far, 0, s)]
                    b = crossed[k][jnp.where(far, s - HALF, 0)]
                    v = jnp.where(far, b, a)
                    if d == 0:
                        got[k][x, j] = v
                    else:
                        back[k][d - 1, j] = v
                    return carry

                lax.fori_loop(0, 4, stage_x, 0)
                if d:
                    second[k] += go(
                        [
                            remote(
                                back[k].at[d - 1],
                                got[k].at[x],
                                s_x2.at[k, d - 1],
                                r_x2.at[k, d - 1],
                                peers[d],
                            )
                        ]
                    )
        if t >= LZ + LX:
            k = t - LZ - LX
            if k == 0:
                pert_copy.wait()
            for c in second[k]:
                c.wait_recv()
            for g in range(4):
                new = got[k][g] + pert_v[:, chan(g), :, lon(k)]
                res4[:, chan(g), :, lon(k)] = new
                strip4[:, chan(g)] = new
            for i, r in enumerate((0, 1, 6, 7)):
                edge[k][i // 2, i % 2] = strip[pl.ds(r, 4 * CH, stride=ROWS)]
            halos[k] = [
                remote(edge[k].at[0], halo.at[1, :, :, lon(k)], s_h.at[k, 0], r_h.at[k, 0], below),
                remote(edge[k].at[1], halo.at[0, :, :, lon(k)], s_h.at[k, 1], r_h.at[k, 1], above),
            ]
            pl.when(dom > 0)(halos[k][0].start)
            pl.when(dom < 31)(halos[k][1].start)
    for k in range(CHUNKS):
        wait_rows(dom, halos[k])
    for c in sent:
        c.wait_send()
    for copies in [masks] + [halos[k] for k in range(CHUNKS)]:
        wait_rows_sent(dom, copies)


def routed(cap, states, pert, sel, listed, mask, coupling, diffusivity, *mine):
    dma = pltpu.SemaphoreType.DMA
    vm = lambda *s: pltpu.VMEM(s, jnp.float32)
    vmem = pl.BlockSpec(memory_space=pltpu.VMEM)
    smem = pl.BlockSpec(memory_space=pltpu.SMEM)
    hbm = pl.BlockSpec(memory_space=pl.ANY)
    scratch = [vm(HALF, GROUP, ROWS, WIDTH)] * (CHUNKS - EARLY)
    for lead in ((cap,), (cap,), (3, 4), (4, 4)):
        scratch += [vm(*lead, GROUP, ROWS, WIDTH)] * CHUNKS
    scratch += [vm(2, 2, 4 * CH, WIDTH)] * CHUNKS
    scratch += [vm(4, CH, ROWS, LON), vm(4 * CH * ROWS, WIDTH)]
    scratch += [pltpu.VMEM((2, ROWS, LON), jnp.int32)]
    three, two, one = dma((CHUNKS, 3)), dma((CHUNKS, 2)), dma((CHUNKS,))
    scratch += [three, three, one, one, one, three, three, two, two, dma((2,)), dma((2,)), dma((1,))]
    return pl.pallas_call(
        functools.partial(route, cap),
        name=f"route{cap}",
        out_shape=(
            jax.ShapeDtypeStruct((4 * CH * ROWS, LON), jnp.float32),
            jax.ShapeDtypeStruct((2, 2, 4 * CH, LON), jnp.float32),
            jax.ShapeDtypeStruct((2, 2 * MIDDLE, OUTER), jnp.bfloat16),
            jax.ShapeDtypeStruct((2, 2 * INNER, MIDDLE), jnp.bfloat16),
            jax.ShapeDtypeStruct((2, MIDDLE, 128), jnp.float32),
            jax.ShapeDtypeStruct((MIDDLE, LON), jnp.float32),
        ),
        in_specs=[hbm, hbm, smem, smem] + [vmem] * (3 + EARLY),
        out_specs=(vmem,) * 6,
        scratch_shapes=scratch,
        compiler_params=pltpu.CompilerParams(
            collective_id=1 + CAPS.index(cap), has_side_effects=True, vmem_limit_bytes=48 << 20
        ),
    )(states, pert, sel, listed, mask, coupling, diffusivity, *mine)


INNER = CH * ROWS
MIDDLE = INNER + 2 * WIN
OUTER = INNER + 4 * WIN


def place(i, off):
    q = i - INNER
    window = (q >= WIN).astype(jnp.int32) + (q >= 2 * WIN) + (q >= 3 * WIN)
    inside = i < INNER
    ch = jnp.where(inside, i >> 3, q - window * WIN - off)
    outer_row = jnp.where(window == 0, -1, jnp.where(window == 1, 8, jnp.where(window == 2, -2, 9)))
    return ch, jnp.where(inside, i & 7, outer_row)


def stencil(coupling, diffusivity, rows, cols, off):
    high = functools.partial(jnp.dot, preferred_element_type=jnp.float32, precision=lax.Precision.HIGHEST)
    ch_a, _ = place(lax.broadcasted_iota(jnp.int32, (rows, CH), 0), off)
    pick_a = (ch_a == lax.broadcasted_iota(jnp.int32, (rows, CH), 1)).astype(jnp.float32)
    ch_b, _ = place(lax.broadcasted_iota(jnp.int32, (CH, cols), 1), off)
    pick_b = (ch_b == lax.broadcasted_iota(jnp.int32, (CH, cols), 0)).astype(jnp.float32)
    full = high(high(pick_a, coupling), pick_b)
    d = jnp.sum(pick_a * diffusivity, axis=1, keepdims=True)
    shape = (rows, cols)
    ci, ri = place(lax.broadcasted_iota(jnp.int32, shape, 0), off)
    cj, rj = place(lax.broadcasted_iota(jnp.int32, shape, 1), off)
    real = (ci >= 0) & (ci < CH) & (cj >= 0) & (cj < CH)
    gap = ri - rj
    vertical = jnp.where(gap == 0, -4.0, jnp.where((gap == 1) | (gap == -1), 1.0, 0.0))
    m = jnp.where(gap == 0, full, 0.0) + jnp.where(ci == cj, vertical * d, 0.0)
    return jnp.where(real, m, 0.0), d


def halves(v):
    top = v.astype(jnp.bfloat16)
    return top, (v - top.astype(jnp.float32)).astype(jnp.bfloat16)


def apply(mat, v):
    dot = functools.partial(jnp.dot, preferred_element_type=jnp.float32)
    top, low = halves(v)
    n = mat.shape[0] // 2
    both = dot(mat[...], top)
    return both[:n] + both[n:] + dot(mat[:n], low)


def build(coupling, diffusivity, odd, mat1, mat2, diff):
    m, d = stencil(coupling, diffusivity, MIDDLE, OUTER, 4 * odd)
    top, low = halves(m)
    mat1[odd, :MIDDLE] = top
    mat1[odd, MIDDLE:] = low
    diff[odd] = jnp.broadcast_to(d, (MIDDLE, 128))
    m, _ = stencil(coupling, diffusivity, INNER, MIDDLE, 4 * odd)
    top, low = halves(m)
    mat2[odd, :INNER] = top
    mat2[odd, INNER:] = low


def sides(v):
    return pltpu.roll(v, 1, 1) + pltpu.roll(v, LON - 1, 1)


def model(res, halo, mat1, mat2, diff, land, out):
    j = pl.program_id(0)

    odd = lax.rem(j, 2)
    start = pl.multiple_of(lax.div(j, 2) * 40 + odd * 16, 8)
    rows = pl.ds(start, WIN)
    v = jnp.concatenate(
        [
            res[0],
            halo[0, 1, rows],
            halo[1, 0, rows],
            halo[0, 0, rows],
            halo[1, 1, rows],
        ],
        axis=0,
    )
    d = diff[odd][:, :1]
    u = v[:MIDDLE]
    first = u + land[...] * (apply(mat1.at[odd], v) + d * sides(u))
    inner = first[:INNER]
    out[0] = inner + land[:INNER] * (apply(mat2.at[odd], first) + d[:INNER] * sides(inner))


def modelled(res, halo, mat1, mat2, diff, land):
    whole = pl.BlockSpec(memory_space=pltpu.VMEM)
    block = pl.BlockSpec((1, INNER, LON), lambda j: (j, 0, 0))
    return pl.pallas_call(
        model,
        name="model",
        grid=(4,),
        out_shape=pltpu.HBM((4, INNER, LON), jnp.float32),
        in_specs=[block, whole, whole, whole, whole, whole],
        out_specs=block,
        compiler_params=pltpu.CompilerParams(vmem_limit_bytes=48 << 20),
    )(res, halo, mat1, mat2, diff, land)


def on_device(states, parents, perturbation, sea_mask, diffusivity, coupling):
    *mine, sel, listed, branch = planned(states, parents)
    res, *others = lax.switch(
        branch[0],
        [functools.partial(routed, cap) for cap in CAPS],
        states,
        perturbation,
        sel,
        listed,
        sea_mask,
        coupling,
        diffusivity[None],
        *mine,
    )
    return modelled(res.reshape(4, INNER, LON), *others).reshape(4, CH, ROWS, LON)


def solution(mesh):
    in_specs = (
        P("particle", None, "domain", None),
        P("particle"),
        P("particle", None, "domain", None),
        P("domain", None),
        P(),
        P(),
    )
    out_specs = P("particle", None, "domain", None)
    return jax.shard_map(
        on_device, mesh=mesh, in_specs=in_specs, out_specs=out_specs, check_vma=False
    )
```

```python
import functools
import jax
import jax.numpy as jnp
from jax import lax
from jax.experimental import pallas as pl
from jax.experimental.pallas import tpu as pltpu
from jax.sharding import PartitionSpec as P

MESH = pl.DeviceIdType.MESH
CH, LON, ROWS = 20, 1024, 8
GROUP = 5
HALF = 16
CAPS = (5, 6, 7, 8, 16)
CHUNKS = 8
WIDTH = LON // CHUNKS
EARLY = 2
AHEAD = 2
LZ, LX = 2, 2
WIN = 24


def remote(src, dst, ss, rs, dev):
    return pltpu.make_async_remote_copy(
        src_ref=src, dst_ref=dst, send_sem=ss, recv_sem=rs, device_id=dev, device_id_type=MESH
    )


def lon(k):
    return pl.ds(k * WIDTH, WIDTH)


def chan(g):
    return pl.ds(g * GROUP, GROUP)


def where_am_i():
    p, dom = lax.axis_index("particle"), lax.axis_index("domain")
    x, h = lax.div(p, 2), lax.rem(p, 2)
    peer_x = [lax.rem(x + d, 4) for d in range(4)]
    peers = [(peer_x[d] * 2 + h, dom) for d in range(4)]
    partner = (x * 2 + 1 - h, dom)
    below, above = (p, lax.rem(dom + 31, 32)), (p, lax.rem(dom + 1, 32))
    return dom, x, h, peer_x, peers, partner, below, above


def meet(devices):
    barrier = pltpu.get_barrier_semaphore()
    for dev in devices:
        pl.semaphore_signal(barrier, inc=1, device_id=dev, device_id_type=MESH)
    pl.semaphore_wait(barrier, len(devices))


def spread(states, mine, k, x, peer_x, peers, ss, rs):
    return [
        remote(
            states.at[:, chan(peer_x[d]), :, lon(k)],
            mine[k].at[pl.ds(x * 4, 4)],
            ss.at[k, d - 1],
            rs.at[k, d - 1],
            peers[d],
        )
        for d in (2, 1, 3)
    ]


def keep(states, mine, k, x, sem):
    return pltpu.make_async_copy(
        states.at[:, chan(x), :, lon(k)], mine[k].at[pl.ds(x * 4, 4)], sem.at[k]
    )


def wait_rows(dom, copies):
    down, up = copies
    pl.when(dom < 31)(down.wait_recv)
    pl.when(dom > 0)(up.wait_recv)


def wait_rows_sent(dom, copies):
    down, up = copies
    pl.when(dom > 0)(down.wait_send)
    pl.when(dom < 31)(up.wait_send)


def plan(states, parents, *refs):
    mine, refs = refs[:EARLY], refs[EARLY:]
    sel, listed, branch, *refs = refs
    par_send, par_x, par_z, par_xs, par_zs, bits, table, *sems = refs
    s_x1, r_x1, l_x1, s_p, r_p, s_q, r_q, l_c = sems
    _, x, h, peer_x, peers, partner, _, _ = where_am_i()
    own = [keep(states, mine, k, x, l_x1) for k in range(EARLY)]
    for c in own:
        c.start()
    lane = lax.broadcasted_iota(jnp.int32, (8, 128), 1)
    row = jnp.zeros((8, 128), jnp.int32)
    for i in range(4):
        row = jnp.where(lane == i, parents[i], row)
    par_send[...] = row
    par_x[pl.ds(x, 1)] = row[None]
    meet(peers[1:] + [partner])

    par = [remote(par_send, par_x.at[x], s_p.at[d - 1], r_p.at[d - 1], peers[d]) for d in range(1, 4)]
    first = sum((spread(states, mine, k, x, peer_x, peers, s_x1, r_x1) for k in range(EARLY)), [])
    for c in par + first:
        c.start()
    for c in par:
        c.wait_recv()
    par2 = remote(par_x, par_z, s_q.at[0], r_q.at[0], partner)
    par2.start()
    to_smem = pltpu.make_async_copy(par_x, par_xs, l_c.at[0])
    to_smem.start()

    def set_bit(i, b):
        bits[i] = b
        return b + b

    lax.fori_loop(0, 32, set_bit, jnp.int32(1))
    to_smem.wait()

    def union(ref):
        return lax.fori_loop(
            0, HALF, lambda i, m: m | bits[ref[lax.div(i, 4), 0, lax.rem(i, 4)]], jnp.int32(0), unroll=4
        )

    def member(l, half):
        return lax.div(l, 4) * 8 + half * 4 + lax.rem(l, 4)

    wanted_here = union(par_xs)

    def arrivals(l, count):
        here, there = member(l, h), member(l, 1 - h)
        table[here] = l
        table[there] = HALF + jnp.minimum(count, HALF - 1)
        return count + (lax.shift_right_logical(wanted_here, there) & 1)

    zero = jnp.int32(0)
    n_in = lax.fori_loop(0, HALF, arrivals, zero, unroll=4)

    def choose(i, carry):
        sel[i] = table[par_xs[lax.div(i, 4), 0, lax.rem(i, 4)]]
        return carry

    lax.fori_loop(0, HALF, choose, 0, unroll=4)
    par2.wait_recv()
    to_smem2 = pltpu.make_async_copy(par_z, par_zs, l_c.at[1])
    to_smem2.start()
    to_smem2.wait()
    wanted_there = union(par_zs)

    def departures(l, carry):
        count, out = carry
        bit = lax.shift_right_logical(wanted_there, member(l, h)) & 1
        out = tuple(
            jnp.where((bit == 1) & (count == c), l, old) for c, old in enumerate(out)
        )
        return count + bit, out

    n_out, out = lax.fori_loop(0, HALF, departures, (zero, (zero,) * HALF), unroll=4)
    for c in range(HALF):
        listed[c] = out[c]
    most = jnp.maximum(n_out, n_in)
    branch[0] = sum((most > cap).astype(jnp.int32) for cap in CAPS[:-1])
    for c in own:
        c.wait()
    for c in par + first:
        c.wait_send()
    for c in first:
        c.wait_recv()
    par2.wait_send()


def planned(states, parents):
    dma = pltpu.SemaphoreType.DMA
    vmem = pl.BlockSpec(memory_space=pltpu.VMEM)
    smem = pl.BlockSpec(memory_space=pltpu.SMEM)
    hbm = pl.BlockSpec(memory_space=pl.ANY)
    shape = jax.ShapeDtypeStruct
    ints = lambda *s: pltpu.SMEM(s, jnp.int32)
    return pl.pallas_call(
        plan,
        name="plan",
        out_shape=[shape((HALF, GROUP, ROWS, WIDTH), jnp.float32)] * EARLY
        + [
            shape((HALF,), jnp.int32),
            shape((HALF,), jnp.int32),
            shape((1,), jnp.int32),
        ],
        in_specs=[hbm, smem],
        out_specs=[vmem] * EARLY + [smem] * 3,
        scratch_shapes=[
            pltpu.VMEM((8, 128), jnp.int32),
            pltpu.VMEM((4, 8, 128), jnp.int32),
            pltpu.VMEM((4, 8, 128), jnp.int32),
            ints(4, 8, 128),
            ints(4, 8, 128),
            ints(32),
            ints(32),
            dma((EARLY, 3)),
            dma((EARLY, 3)),
            dma((EARLY,)),
            dma((3,)),
            dma((3,)),
            dma((1,)),
            dma((1,)),
            dma((2,)),
        ],
        compiler_params=pltpu.CompilerParams(
            collective_id=0, has_side_effects=True, vmem_limit_bytes=48 << 20
        ),
    )(states, parents)


def route(cap, states, pert, sel, listed, mask, coupling, diffusivity, *refs):
    mine, refs = refs[:EARLY], refs[EARLY:]
    res, halo, mat1, mat2, diff, land, *refs = refs
    it = iter(refs)
    take = lambda n: [next(it) for _ in range(n)]
    mine = list(mine) + take(CHUNKS - EARLY)
    crossing, crossed, back, got, edge = (take(CHUNKS) for _ in range(5))
    pert_v, strip, mask_halo = take(3)
    s_x1, r_x1, l_x1, s_z, r_z, s_x2, r_x2, s_h, r_h, s_m, r_m, l_c = it
    dom, x, h, peer_x, peers, partner, below, above = where_am_i()
    own = {k: keep(states, mine, k, x, l_x1) for k in range(EARLY, CHUNKS)}
    for c in own.values():
        c.start()
    pert_copy = pltpu.make_async_copy(pert, pert_v, l_c.at[0])
    pert_copy.start()

    @pl.when(dom == 0)
    def _():
        halo[0] = jnp.zeros(halo.shape[1:], jnp.float32)
        mask_halo[0] = jnp.zeros(mask_halo.shape[1:], jnp.int32)

    @pl.when(dom == 31)
    def _():
        halo[1] = jnp.zeros(halo.shape[1:], jnp.float32)
        mask_halo[1] = jnp.zeros(mask_halo.shape[1:], jnp.int32)

    masks = [
        remote(mask, mask_halo.at[1], s_m.at[0], r_m.at[0], below),
        remote(mask, mask_halo.at[0], s_m.at[1], r_m.at[1], above),
    ]
    sent = []

    def go(copies):
        for c in copies:
            c.start()
        sent.extend(copies)
        return copies

    def stage_z(k):
        def body(c, carry):
            crossing[k][c] = mine[k][listed[c]]
            return carry

        lax.fori_loop(0, cap, body, 0)

    stage_z(0)
    meet(peers[1:] + [partner, below, above])
    x1 = lambda k: go(spread(states, mine, k, x, peer_x, peers, s_x1, r_x1))
    first = {}
    res4 = res.reshape(4, CH, ROWS, LON)
    strip4 = strip.reshape(4, CH, ROWS, WIDTH)
    z, second, halos = {}, {}, {}
    for t in range(CHUNKS + LZ + LX):
        if t < CHUNKS:
            k = t
            if k >= EARLY:
                own[k].wait()
                for c in first[k]:
                    c.wait_recv()
            if k:
                stage_z(k)
            z[k] = go([remote(crossing[k], crossed[k], s_z.at[k], r_z.at[k], partner)])
            for j in range(EARLY, AHEAD + 1) if k == 0 else [k + AHEAD]:
                if j < CHUNKS:
                    first[j] = x1(j)
        if t == 0:
            pl.when(dom > 0)(masks[0].start)
            pl.when(dom < 31)(masks[1].start)
        if t == 1:
            for odd in range(2):
                build(coupling[...], diffusivity[...], odd, mat1, mat2, diff)
            wait_rows(dom, masks)
            sea = mask[...].astype(jnp.float32)
            for c in range(CH):
                land[pl.ds(c * ROWS, ROWS)] = sea
            low = mask_halo[0, ROWS - 1 : ROWS].astype(jnp.float32)
            high = mask_halo[1, 0:1].astype(jnp.float32)
            land[pl.ds(INNER, WIN)] = jnp.broadcast_to(low, (WIN, LON))
            land[pl.ds(INNER + WIN, WIN)] = jnp.broadcast_to(high, (WIN, LON))
        if LZ <= t < CHUNKS + LZ:
            k = t - LZ
            z[k][0].wait_recv()
            second[k] = []
            for d in (2, 1, 3, 0):

                def stage_x(j, carry, k=k, d=d):
                    s = sel[peer_x[d] * 4 + j]
                    far = s >= HALF
                    a = mine[k][jnp.where(far, 0, s)]
                    b = crossed[k][jnp.where(far, s - HALF, 0)]
                    v = jnp.where(far, b, a)
                    if d == 0:
                        got[k][x, j] = v
                    else:
                        back[k][d - 1, j] = v
                    return carry

                lax.fori_loop(0, 4, stage_x, 0)
                if d:
                    second[k] += go(
                        [
                            remote(
                                back[k].at[d - 1],
                                got[k].at[x],
                                s_x2.at[k, d - 1],
                                r_x2.at[k, d - 1],
                                peers[d],
                            )
                        ]
                    )
        if t >= LZ + LX:
            k = t - LZ - LX
            if k == 0:
                pert_copy.wait()
            for c in second[k]:
                c.wait_recv()
            for g in range(4):
                new = got[k][g] + pert_v[:, chan(g), :, lon(k)]
                res4[:, chan(g), :, lon(k)] = new
                strip4[:, chan(g)] = new
            for i, r in enumerate((0, 1, 6, 7)):
                edge[k][i // 2, i % 2] = strip[pl.ds(r, 4 * CH, stride=ROWS)]
            halos[k] = [
                remote(edge[k].at[0], halo.at[1, :, :, lon(k)], s_h.at[k, 0], r_h.at[k, 0], below),
                remote(edge[k].at[1], halo.at[0, :, :, lon(k)], s_h.at[k, 1], r_h.at[k, 1], above),
            ]
            pl.when(dom > 0)(halos[k][0].start)
            pl.when(dom < 31)(halos[k][1].start)
    for k in range(CHUNKS):
        wait_rows(dom, halos[k])
    for c in sent:
        c.wait_send()
    for copies in [masks] + [halos[k] for k in range(CHUNKS)]:
        wait_rows_sent(dom, copies)


def routed(cap, states, pert, sel, listed, mask, coupling, diffusivity, *mine):
    dma = pltpu.SemaphoreType.DMA
    vm = lambda *s: pltpu.VMEM(s, jnp.float32)
    vmem = pl.BlockSpec(memory_space=pltpu.VMEM)
    smem = pl.BlockSpec(memory_space=pltpu.SMEM)
    hbm = pl.BlockSpec(memory_space=pl.ANY)
    scratch = [vm(HALF, GROUP, ROWS, WIDTH)] * (CHUNKS - EARLY)
    for lead in ((cap,), (cap,), (3, 4), (4, 4)):
        scratch += [vm(*lead, GROUP, ROWS, WIDTH)] * CHUNKS
    scratch += [vm(2, 2, 4 * CH, WIDTH)] * CHUNKS
    scratch += [vm(4, CH, ROWS, LON), vm(4 * CH * ROWS, WIDTH)]
    scratch += [pltpu.VMEM((2, ROWS, LON), jnp.int32)]
    three, two, one = dma((CHUNKS, 3)), dma((CHUNKS, 2)), dma((CHUNKS,))
    scratch += [three, three, one, one, one, three, three, two, two, dma((2,)), dma((2,)), dma((1,))]
    return pl.pallas_call(
        functools.partial(route, cap),
        name=f"route{cap}",
        out_shape=(
            jax.ShapeDtypeStruct((4 * CH * ROWS, LON), jnp.float32),
            jax.ShapeDtypeStruct((2, 2, 4 * CH, LON), jnp.float32),
            jax.ShapeDtypeStruct((2, 2 * MIDDLE, OUTER), jnp.bfloat16),
            jax.ShapeDtypeStruct((2, 2 * INNER, MIDDLE), jnp.bfloat16),
            jax.ShapeDtypeStruct((2, MIDDLE, 128), jnp.float32),
            jax.ShapeDtypeStruct((MIDDLE, LON), jnp.float32),
        ),
        in_specs=[hbm, hbm, smem, smem] + [vmem] * (3 + EARLY),
        out_specs=(vmem,) * 6,
        scratch_shapes=scratch,
        compiler_params=pltpu.CompilerParams(
            collective_id=1 + CAPS.index(cap), has_side_effects=True, vmem_limit_bytes=48 << 20
        ),
    )(states, pert, sel, listed, mask, coupling, diffusivity, *mine)


INNER = CH * ROWS
MIDDLE = INNER + 2 * WIN
OUTER = INNER + 4 * WIN


def place(i, off):
    q = i - INNER
    window = (q >= WIN).astype(jnp.int32) + (q >= 2 * WIN) + (q >= 3 * WIN)
    inside = i < INNER
    ch = jnp.where(inside, i >> 3, q - window * WIN - off)
    outer_row = jnp.where(window == 0, -1, jnp.where(window == 1, 8, jnp.where(window == 2, -2, 9)))
    return ch, jnp.where(inside, i & 7, outer_row)


def stencil(coupling, diffusivity, rows, cols, off):
    high = functools.partial(jnp.dot, preferred_element_type=jnp.float32, precision=lax.Precision.HIGHEST)
    ch_a, _ = place(lax.broadcasted_iota(jnp.int32, (rows, CH), 0), off)
    pick_a = (ch_a == lax.broadcasted_iota(jnp.int32, (rows, CH), 1)).astype(jnp.float32)
    ch_b, _ = place(lax.broadcasted_iota(jnp.int32, (CH, cols), 1), off)
    pick_b = (ch_b == lax.broadcasted_iota(jnp.int32, (CH, cols), 0)).astype(jnp.float32)
    full = high(high(pick_a, coupling), pick_b)
    d = jnp.sum(pick_a * diffusivity, axis=1, keepdims=True)
    shape = (rows, cols)
    ci, ri = place(lax.broadcasted_iota(jnp.int32, shape, 0), off)
    cj, rj = place(lax.broadcasted_iota(jnp.int32, shape, 1), off)
    real = (ci >= 0) & (ci < CH) & (cj >= 0) & (cj < CH)
    gap = ri - rj
    vertical = jnp.where(gap == 0, -4.0, jnp.where((gap == 1) | (gap == -1), 1.0, 0.0))
    m = jnp.where(gap == 0, full, 0.0) + jnp.where(ci == cj, vertical * d, 0.0)
    return jnp.where(real, m, 0.0), d


def halves(v):
    top = v.astype(jnp.bfloat16)
    return top, (v - top.astype(jnp.float32)).astype(jnp.bfloat16)


def apply(mat, v):
    dot = functools.partial(jnp.dot, preferred_element_type=jnp.float32)
    top, low = halves(v)
    n = mat.shape[0] // 2
    both = dot(mat[...], top)
    return both[:n] + both[n:] + dot(mat[:n], low)


def build(coupling, diffusivity, odd, mat1, mat2, diff):
    m, d = stencil(coupling, diffusivity, MIDDLE, OUTER, 4 * odd)
    top, low = halves(m)
    mat1[odd, :MIDDLE] = top
    mat1[odd, MIDDLE:] = low
    diff[odd] = jnp.broadcast_to(d, (MIDDLE, 128))
    m, _ = stencil(coupling, diffusivity, INNER, MIDDLE, 4 * odd)
    top, low = halves(m)
    mat2[odd, :INNER] = top
    mat2[odd, INNER:] = low


def sides(v):
    return pltpu.roll(v, 1, 1) + pltpu.roll(v, LON - 1, 1)


def model(res, halo, mat1, mat2, diff, land, out):
    j = pl.program_id(0)

    odd = lax.rem(j, 2)
    start = pl.multiple_of(lax.div(j, 2) * 40 + odd * 16, 8)
    rows = pl.ds(start, WIN)
    v = jnp.concatenate(
        [
            res[0],
            halo[0, 1, rows],
            halo[1, 0, rows],
            halo[0, 0, rows],
            halo[1, 1, rows],
        ],
        axis=0,
    )
    d = diff[odd][:, :1]
    u = v[:MIDDLE]
    first = u + land[...] * (apply(mat1.at[odd], v) + d * sides(u))
    inner = first[:INNER]
    out[0] = inner + land[:INNER] * (apply(mat2.at[odd], first) + d[:INNER] * sides(inner))


def modelled(res, halo, mat1, mat2, diff, land):
    whole = pl.BlockSpec(memory_space=pltpu.VMEM)
    block = pl.BlockSpec((1, INNER, LON), lambda j: (j, 0, 0))
    return pl.pallas_call(
        model,
        name="model",
        grid=(4,),
        out_shape=pltpu.HBM((4, INNER, LON), jnp.float32),
        in_specs=[block, whole, whole, whole, whole, whole],
        out_specs=block,
        compiler_params=pltpu.CompilerParams(vmem_limit_bytes=48 << 20),
    )(res, halo, mat1, mat2, diff, land)


def on_device(states, parents, perturbation, sea_mask, diffusivity, coupling):
    *mine, sel, listed, branch = planned(states, parents)
    res, *others = lax.switch(
        branch[0],
        [functools.partial(routed, cap) for cap in CAPS],
        states,
        perturbation,
        sel,
        listed,
        sea_mask,
        coupling,
        diffusivity[None],
        *mine,
    )
    return modelled(res.reshape(4, INNER, LON), *others).reshape(4, CH, ROWS, LON)


def solution(mesh):
    in_specs = (
        P("particle", None, "domain", None),
        P("particle"),
        P("particle", None, "domain", None),
        P("domain", None),
        P(),
        P(),
    )
    out_specs = P("particle", None, "domain", None)
    return jax.shard_map(
        on_device, mesh=mesh, in_specs=in_specs, out_specs=out_specs, check_vma=False
    )
```
